256 devices in a mesh: dp: 8 (over x, y_hi), ctx: 32 (over z, y_lo, core).
Axes of the slice: x: 4, y: 4 (y_hi: 2, y_lo: 2; y = y_hi * 2 + y_lo), z: 8, core: 2. Of those that a mesh axis runs over, the one named last changes fastest.
Arguments:
- queries: bfloat16 [8, 4096, 2048], P('dp', 'ctx'), may hold values from -6 to 6
- key_states: bfloat16 [8, 4096, 2048], P('dp', 'ctx'), may hold values from -6 to 6
- value_states: bfloat16 [8, 4096, 2048], P('dp', 'ctx'), may hold values from -6 to 6
- cotangent: bfloat16 [8, 4096, 2048], P('dp', 'ctx'), may hold values from -6 to 6
- signal: bfloat16 [8, 4096, 128], P('dp', 'ctx'), may hold values from -1500 to 1500
- signal_weight: bfloat16 [2, 128, 4096], replicated, may hold values from -0.5 to 0.5
- embodiment: int32 [8, 4096], P('dp', 'ctx'), may hold values from 0 to 15
- token_type: int32 [8, 4096], P('dp', 'ctx'), may hold values from 0 to 2
- earliest: int32 [8, 4096], P('dp', 'ctx'), may hold values from 0 to 4095, as said below
- prior_mean: float32 [16, 128], replicated, may hold values from -4 to 4
- prior_var: float32 [16, 128], replicated, may hold values from 0.5 to 4
- prior_count: float32 [16], replicated, may hold values from 1000 to 8000
Outputs:
- attended: bfloat16 [8, 4096, 2048], P('dp', 'ctx')
- d_queries: bfloat16 [8, 4096, 2048], P('dp', 'ctx')
- d_keys: bfloat16 [8, 4096, 2048], P('dp', 'ctx')
- d_values: bfloat16 [8, 4096, 2048], P('dp', 'ctx')
- d_signal_weight: bfloat16 [2, 128, 4096], replicated
The draws below stay inside these ranges and needn't reach their ends.
Inputs may be any that keep to these rules, and one draw needn't show every extreme that they name: In every episode, max(0, t - 384) <= earliest[t] <= t for position t, and the lower bound t - 384 is reached in every draw.
All inputs are finite; a program needn't handle non-finite values.
Results may differ from the reference program's by a relative error of at most 0.005.
The reference program's roundings to bfloat16 on the way (of `stacked`, `probs_low`, `dscore` and `d_embed`) count: a program that leaves them out, or rounds other values in their place, can miss the bound.
Values may be sent and summed in bfloat16 or wider, within the bound.
No kernel may reach another device: no remote copies, remote signals or barrier semaphores. Data moves between devices by JAX's collectives and lax.ppermute only.
A program may use at most 128 MiB of HBM per device.

```python
import math
import jax
import jax.numpy as jnp
from jax import lax

HEADS = 16
HEAD_DIM = 128
F = 128
E = 16
T_DEV = 128
HOPS = 3
EPISODES = 8
LENGTH = 4096
N_CTX = 32


def draw_queries(key, part):
    key = jax.random.fold_in(key, 11)
    shape = (EPISODES, LENGTH, HEADS * HEAD_DIM)
    base = jnp.clip(jax.random.normal(key, shape, jnp.float32), -6.0, 6.0)
    return base.astype(jnp.bfloat16)


def draw_key_states(key, part):
    key = jax.random.fold_in(key, 12)
    shape = (EPISODES, LENGTH, HEADS * HEAD_DIM)
    base = jnp.clip(jax.random.normal(key, shape, jnp.float32), -6.0, 6.0)
    return base.astype(jnp.bfloat16)


def draw_signal(key, part):
    key = jax.random.fold_in(key, 13)
    key_col, key_row, key_noise = jax.random.split(key, 3)
    shape = (EPISODES, LENGTH, F)
    column = jnp.exp(jax.random.uniform(key_col, (F,), jnp.float32) * math.log(10.0))
    rowwise = jnp.exp(jax.random.uniform(key_row, (EPISODES, LENGTH, 1), jnp.float32) * math.log(4.0))
    trend = (1.0 + 2.0 * jnp.arange(LENGTH, dtype=jnp.float32) / LENGTH)[None, :, None]
    trend = trend * (1.0 + jnp.arange(EPISODES, dtype=jnp.float32) / EPISODES)[:, None, None]
    noise = jnp.clip(jax.random.normal(key_noise, shape, jnp.float32), -4.0, 4.0)
    return (noise * column * rowwise * trend).astype(jnp.bfloat16)


def draw_earliest(key, part):
    key = jax.random.fold_in(key, 17)
    position = jnp.arange(LENGTH, dtype=jnp.int32)[None, :]
    reach = jax.random.randint(key, (EPISODES, LENGTH), 0, HOPS * T_DEV + 1, jnp.int32)
    reach = jnp.where(position % T_DEV == T_DEV - 1, HOPS * T_DEV, reach)
    return jnp.maximum(position - reach, 0).astype(jnp.int32)


def plant(values, own_key, least, largest):
    index_at = [jax.random.randint(jax.random.fold_in(own_key, axis), (), 0, length) for axis, length in enumerate(values.shape)]
    main_axis = values.shape.index(max(values.shape))
    beside = index_at[:main_axis] + [(index_at[main_axis] + 1) % values.shape[main_axis]] + index_at[main_axis + 1:]
    return values.at[tuple(index_at)].set(least).at[tuple(beside)].set(largest)


def block_scale(own_key, extent, cuts, least, high):
    loudness, own = 1.0, jax.random.fold_in(own_key, 6)
    for dim, shards_of in cuts:
        steps = jnp.exp(jax.random.uniform(jax.random.fold_in(own, dim), (shards_of,), jnp.float32, least / len(cuts), high / len(cuts)))
        loudness = loudness * jnp.repeat(steps, extent[dim] // shards_of).reshape([-1 if axis == dim else 1 for axis in range(len(extent))])
    return loudness


def centred(own_key, extent, width, bound, cuts=(), kind=jnp.bfloat16):
    factor_of = block_scale(own_key, extent, cuts, -0.22, 0.18) if cuts else 1.0
    result = jax.random.normal(own_key, extent, jnp.float32) * width * factor_of
    return jnp.minimum(jnp.maximum(result, -bound), bound).astype(kind)


def setup_inputs(seed: int = 0) -> dict:
    seeds = jax.random.split(jax.random.key(seed), 13)
    queries = draw_queries(jax.random.fold_in(seeds[12], 71), 0)
    key_states = draw_key_states(jax.random.fold_in(seeds[12], 71), 0)
    value_states = centred(seeds[2], (EPISODES, LENGTH, HEADS * HEAD_DIM), 1.0, 6.0, ((0, 8), (1, 32)))
    cotangent = centred(seeds[3], (EPISODES, LENGTH, HEADS * HEAD_DIM), 1.0, 6.0, ((0, 8), (1, 32)))
    signal = draw_signal(jax.random.fold_in(seeds[12], 71), 0)
    signal_weight = centred(seeds[5], (2, F, 2 * HEADS * HEAD_DIM), F ** -0.5, 0.5)
    embodiment = plant(jax.random.randint(seeds[6], (EPISODES, LENGTH), 0, E), jax.random.fold_in(seeds[6], 1), 0, E - 1).astype(jnp.int32)
    token_type = plant(jax.random.randint(seeds[7], (EPISODES, LENGTH), 0, 3), jax.random.fold_in(seeds[7], 1), 0, 2).astype(jnp.int32)
    earliest = draw_earliest(jax.random.fold_in(seeds[12], 71), 0)
    prior_mean = centred(seeds[9], (E, F), 1.0, 4.0, (), jnp.float32)
    prior_var = jnp.clip(jnp.exp(jax.random.uniform(seeds[10], (E, F), jnp.float32, math.log(0.5), math.log(4.0))), 0.5, 4.0)
    prior_count = jnp.clip(jnp.exp(jax.random.uniform(seeds[11], (E,), jnp.float32, math.log(1000.0), math.log(8000.0))), 1000.0, 8000.0)
    return dict(queries=queries, key_states=key_states, value_states=value_states, cotangent=cotangent, signal=signal, signal_weight=signal_weight, embodiment=embodiment, token_type=token_type, earliest=earliest, prior_mean=prior_mean, prior_var=prior_var, prior_count=prior_count)


norm_eps = 1e-05
high_prec = lax.Precision.HIGHEST

def head_groups(query_rows, key_win, value_win, grad_rows, visible):
    row_count = query_rows.shape[0]
    span_rows = key_win.shape[0]
    group_size = math.gcd(4, HEADS)
    group_count = HEADS // group_size
    score_scale = 1.0 / math.sqrt(HEAD_DIM)

    def split_heads(array_in, length_rows):
        return jnp.moveaxis(array_in.reshape(length_rows, group_count, group_size, HEAD_DIM), 1, 0)

    def group_step(group_parts):
        query_g, key_g, value_g, grad_g = [part.astype(jnp.float32) for part in group_parts]
        scores = jnp.einsum('thd,whd->htw', query_g, key_g) * score_scale
        scores = jnp.where(visible[None], scores, jnp.float32(-1e+30))
        row_max = lax.optimization_barrier(jnp.max(scores, axis=-1, keepdims=True))
        exponent = jnp.exp(scores - row_max)
        probs_full = exponent / lax.optimization_barrier(jnp.sum(exponent, axis=-1, keepdims=True))
        probs_low = probs_full.astype(jnp.bfloat16).astype(jnp.float32)
        output = jnp.einsum('htw,whd->thd', probs_low, value_g)
        dprobs = jnp.einsum('thd,whd->htw', grad_g, value_g)
        dvalue = jnp.einsum('htw,thd->whd', probs_low, grad_g)
        inner_sum = lax.optimization_barrier(jnp.sum(probs_full * dprobs, axis=-1, keepdims=True))
        dscore = (probs_full * (dprobs - inner_sum)).astype(jnp.bfloat16).astype(jnp.float32)
        dquery = jnp.einsum('htw,whd->thd', dscore, key_g) * score_scale
        key_grad = jnp.einsum('htw,thd->whd', dscore, query_g) * score_scale
        return (output.astype(jnp.bfloat16), dquery.astype(jnp.bfloat16), key_grad, dvalue)
    results = lax.map(group_step, (split_heads(query_rows, row_count), split_heads(key_win, span_rows), split_heads(value_win, span_rows), split_heads(grad_rows, row_count)))

    def join_heads(array_in, length_rows):
        return jnp.moveaxis(array_in, 0, 1).reshape(length_rows, HEADS * HEAD_DIM)
    return (join_heads(results[0], row_count), join_heads(results[1], row_count), join_heads(results[2], span_rows), join_heads(results[3], span_rows))

def reference(queries, key_states, value_states, cotangent, signal, signal_weight, embodiment, token_type, earliest, prior_mean, prior_var, prior_count):
    model_width = HEADS * HEAD_DIM
    sig_values = signal.astype(jnp.float32).reshape(-1, F)
    kind_row = token_type.reshape(-1)
    sig_mask = (kind_row < 2).astype(jnp.float32)
    onehot = (embodiment.reshape(-1)[:, None] == jnp.arange(E, dtype=jnp.int32)[None, :]).astype(jnp.float32)
    picked = onehot * sig_mask[:, None]
    counts = lax.optimization_barrier(jnp.sum(picked, axis=0))
    sum_first = jnp.dot(picked.T, sig_values, precision=high_prec)
    second = jnp.dot(picked.T, sig_values * sig_values, precision=high_prec)
    total_weight = prior_count + counts
    new_mean = (prior_count[:, None] * prior_mean + sum_first) / total_weight[:, None]
    new_square = (prior_count[:, None] * (prior_var + prior_mean * prior_mean) + second) / total_weight[:, None]
    inv_std = lax.rsqrt(new_square - new_mean * new_mean + norm_eps)
    token_mean = jnp.dot(onehot, new_mean, precision=high_prec)
    token_inv = jnp.dot(onehot, inv_std, precision=high_prec)
    normed = (sig_values - token_mean) * token_inv
    stacked = jnp.concatenate([normed * (kind_row == 0).astype(jnp.float32)[:, None], normed * (kind_row == 1).astype(jnp.float32)[:, None]], axis=1).astype(jnp.bfloat16)
    embedded = jnp.dot(stacked, signal_weight.reshape(2 * F, 2 * model_width), preferred_element_type=jnp.float32)
    key_rows = (key_states.reshape(-1, model_width) + embedded[:, :model_width]).astype(jnp.bfloat16).reshape(EPISODES, LENGTH, model_width)
    value_rows = (value_states.reshape(-1, model_width) + embedded[:, model_width:]).astype(jnp.bfloat16).reshape(EPISODES, LENGTH, model_width)
    span_rows = (HOPS + 1) * T_DEV
    padding = HOPS * T_DEV

    def episode_fn(inputs):
        query_ep, key_ep, value_ep, grad_ep, early_ep = inputs
        blank = jnp.zeros((padding, model_width), jnp.bfloat16)
        key_pad = jnp.concatenate([blank, key_ep], axis=0)
        value_pad = jnp.concatenate([blank, value_ep], axis=0)

        def block_step(grads, block_id):
            start = (block_id * T_DEV).astype(jnp.int32)
            query_blk = lax.dynamic_slice_in_dim(query_ep, start, T_DEV, 0)
            grad_blk = lax.dynamic_slice_in_dim(grad_ep, start, T_DEV, 0)
            key_win = lax.dynamic_slice_in_dim(key_pad, start, span_rows, 0)
            value_win = lax.dynamic_slice_in_dim(value_pad, start, span_rows, 0)
            early = lax.dynamic_slice_in_dim(early_ep, start, T_DEV, 0)
            query_pos = start + jnp.arange(T_DEV, dtype=jnp.int32)
            key_pos = start - padding + jnp.arange(span_rows, dtype=jnp.int32)
            visible = (key_pos[None, :] >= early[:, None]) & (key_pos[None, :] <= query_pos[:, None])
            output, dquery, key_grad, dvalue = head_groups(query_blk, key_win, value_win, grad_blk, visible)
            current = lax.dynamic_slice_in_dim(grads, start, span_rows, 1)
            grads = lax.dynamic_update_slice_in_dim(grads, current + jnp.stack((key_grad, dvalue)), start, 1)
            return (grads, (output, dquery))
        start_grads = jnp.zeros((2, padding + LENGTH, model_width), jnp.float32)
        grads, (outputs, dqueries) = lax.scan(block_step, start_grads, jnp.arange(N_CTX, dtype=jnp.int32))
        return (outputs.reshape(LENGTH, model_width), dqueries.reshape(LENGTH, model_width), grads[:, padding:])
    attended, d_queries, grads = lax.map(episode_fn, (queries, key_rows, value_rows, cotangent, earliest))
    d_embed = jnp.concatenate([grads[:, 0], grads[:, 1]], axis=-1).reshape(-1, 2 * model_width).astype(jnp.bfloat16)
    partial_term = jnp.dot(stacked.T, d_embed, preferred_element_type=jnp.float32)
    d_weight = (partial_term * (1.0 / math.sqrt(EPISODES * LENGTH))).astype(jnp.bfloat16).reshape(2, F, 2 * model_width)
    return (attended, d_queries, grads[:, 0].astype(jnp.bfloat16), grads[:, 1].astype(jnp.bfloat16), d_weight)
```

```python
import math

import jax
import jax.numpy as jnp
from jax import lax
from jax.experimental import pallas as pl
from jax.experimental.pallas import tpu as pltpu
from jax.sharding import Mesh
from jax.sharding import PartitionSpec as P

D = 128
F = 128
E = 16
T = 128
HOPS = 3
G = 4
BAND = (HOPS + 1) * T
WIN = HOPS + G
STAT_ROWS = 2 * E + 8
NORM_EPS = 1e-5
LOG2E = math.log2(math.e)

bf16, f32 = jnp.bfloat16, jnp.float32
NN = (((1,), (0,)), ((), ()))
NT = (((1,), (1,)), ((), ()))
TN = (((0,), (0,)), ((), ()))


def dot(a, b, dims=NN):
    return lax.dot_general(a, b, dims, preferred_element_type=f32)


def stats_kernel(sig_ref, emb_ref, typ_ref, out_ref):
    sig = sig_ref[...]
    picked = (lax.broadcasted_iota(jnp.int32, (T, T), 0) == emb_ref[...]) & (typ_ref[...] < 2)
    pick = jnp.where(picked, 1.0, 0.0).astype(bf16)
    square = sig.astype(f32) * sig.astype(f32)
    high = square.astype(bf16)
    low = (square - high.astype(f32)).astype(bf16)
    first = dot(pick[:E], sig)
    second = dot(pick[:E], high) + dot(pick[:E], low)
    counts = dot(jnp.ones((8, T), bf16), pick, NT)
    for copy in range(out_ref.shape[0]):
        out_ref[copy, 0:E] = first
        out_ref[copy, E : 2 * E] = second
        out_ref[copy, 2 * E :] = counts


def resum_kernel(in_ref, out_ref):
    total = in_ref[0]
    for part in range(1, in_ref.shape[0]):
        total = total + in_ref[part]
    for copy in range(out_ref.shape[0]):
        out_ref[copy] = total


def split3(value):
    high = value.astype(bf16)
    rest = value - high.astype(f32)
    mid = rest.astype(bf16)
    return high, mid, (rest - mid.astype(f32)).astype(bf16)


def main_kernel(
    stat_ref, pmean_ref, pvar_ref, pcount_ref, sig_h_ref, sig_o_ref,
    kh_ref, ko_ref, vh_ref, vo_ref, q_ref, g_ref, wk_ref, wv_ref,
    att_ref, dq_ref, dkh_ref, dko_ref, dvh_ref, dvo_ref, dw_ref,
    stacked_ref, stacked_t_ref, bias_ref, k_ref, v_ref, dk_ref, dv_ref,
):
    scale = 1.0 / math.sqrt(D)

    @pl.when(pl.program_id(0) == 0)
    def _():
        stat = stat_ref[0]
        for part in range(1, stat_ref.shape[0]):
            stat = stat + stat_ref[part]
        diag = lax.broadcasted_iota(jnp.int32, (E, T), 0) == lax.broadcasted_iota(
            jnp.int32, (E, T), 1
        )
        counts = jnp.sum(
            jnp.where(diag, jnp.broadcast_to(stat[2 * E : 2 * E + 1], (E, T)), 0.0),
            axis=1, keepdims=True,
        )
        prior = jnp.sum(
            jnp.where(diag, jnp.broadcast_to(pcount_ref[...], (E, T)), 0.0), axis=1, keepdims=True
        )
        pmean = pmean_ref[...]
        total = prior + counts
        mean = (prior * pmean + stat[0:E]) / total
        square = (prior * (pvar_ref[...] + pmean * pmean) + stat[E : 2 * E]) / total
        inv = lax.rsqrt(square - mean * mean + NORM_EPS)
        zero = jnp.zeros_like(inv)
        table = jnp.concatenate(
            [
                jnp.concatenate([mean, inv, zero], axis=1),
                jnp.concatenate([mean, zero, inv], axis=1),
            ],
            axis=0,
        )
        pieces = split3(table)
        row = lax.broadcasted_iota(jnp.int32, (2 * E, T), 0)
        for b in range(WIN):
            src = sig_h_ref[b] if b < HOPS else sig_o_ref[b - HOPS]
            info = src[T : T + 16].astype(f32)
            code = (info[0:1] + E * info[1:2]).astype(jnp.int32)
            pick = jnp.where(row == code, 1.0, 0.0).astype(bf16)
            per_token = dot(pick, pieces[0], TN) + dot(pick, pieces[1], TN) + dot(pick, pieces[2], TN)
            centred = src[0:T].astype(f32) - per_token[:, 0:F]
            stacked = jnp.concatenate(
                [centred * per_token[:, F : 2 * F], centred * per_token[:, 2 * F :]], axis=1
            )
            stacked_ref[b * T : (b + 1) * T] = stacked.astype(bf16)
            stacked_t_ref[:, b * T : (b + 1) * T] = stacked.T.astype(bf16)
        key_row = lax.broadcasted_iota(jnp.int32, (BAND, T), 0)
        last = lax.broadcasted_iota(jnp.int32, (BAND, T), 1) + HOPS * T
        for b in range(G):
            info = sig_o_ref[b][T : T + 16].astype(f32)
            reach = (16.0 * info[2:3] + info[3:4]).astype(jnp.int32)
            visible = (key_row <= last) & (key_row >= last - reach)
            bias_ref[b] = jnp.where(visible, 0.0, -1e30)

    embed_k = dot(stacked_ref[...], wk_ref[...])
    embed_v = dot(stacked_ref[...], wv_ref[...])
    for b in range(WIN):
        rows = slice(b * T, (b + 1) * T)
        raw_k = kh_ref[b] if b < HOPS else ko_ref[b - HOPS]
        raw_v = vh_ref[b] if b < HOPS else vo_ref[b - HOPS]
        k_ref[rows] = (raw_k.astype(f32) + embed_k[rows]).astype(bf16)
        v_ref[rows] = (raw_v.astype(f32) + embed_v[rows]).astype(bf16)
    for b in range(G):
        band = slice(b * T, b * T + BAND)
        q, g = q_ref[b], g_ref[b]
        key, value = k_ref[band], v_ref[band]
        score = dot(key, q, NT) * (scale * LOG2E) + bias_ref[b]
        expo = jnp.exp2(score - jnp.max(score, axis=0, keepdims=True))
        probs = expo * (1.0 / jnp.sum(expo, axis=0, keepdims=True))
        probs_low = probs.astype(bf16)
        dprobs = dot(value, g, NT)
        inner = jnp.sum(probs * dprobs, axis=0, keepdims=True)
        dscore = (probs * (dprobs - inner)).astype(bf16)
        att_ref[b] = dot(probs_low, value, TN).astype(bf16)
        dq_ref[b] = (dot(dscore, key, TN) * scale).astype(bf16)
        dkey = dot(dscore, q) * scale
        dvalue = dot(probs_low, g)
        if b == 0:
            dk_ref[band], dv_ref[band] = dkey, dvalue
        else:
            old = slice(b * T, b * T + BAND - T)
            new = slice(b * T + BAND - T, b * T + BAND)
            dk_ref[old] += dkey[: BAND - T]
            dv_ref[old] += dvalue[: BAND - T]
            dk_ref[new] = dkey[BAND - T :]
            dv_ref[new] = dvalue[BAND - T :]
    for b in range(WIN):
        rows = slice(b * T, (b + 1) * T)
        if b < HOPS:
            dkh_ref[b] = dk_ref[rows].astype(bf16)
            dvh_ref[b] = dv_ref[rows].astype(bf16)
        else:
            dko_ref[b - HOPS] = dk_ref[rows]
            dvo_ref[b - HOPS] = dv_ref[rows]
    dw_ref[0, 0] = dot(stacked_t_ref[...], dk_ref[...].astype(bf16)).astype(bf16)
    dw_ref[1, 0] = dot(stacked_t_ref[...], dv_ref[...].astype(bf16)).astype(bf16)


def main_call(stat, pmean, pvar, pcount, sig_h, sig_o, kh, ko, vh, vo, q, g, wk, wv):
    heads = ko.shape[2] // D
    whole = lambda a: pl.BlockSpec(a.shape, lambda h: (0,) * a.ndim)
    part = lambda n: pl.BlockSpec((n, T, D), lambda h: (0, 0, h))
    wide = pl.BlockSpec((2 * F, D), lambda h: (0, h))
    shape = lambda n, t: jax.ShapeDtypeStruct((n, T, heads * D), t)
    return pl.pallas_call(
        main_kernel,
        grid=(heads,),
        in_specs=[
            whole(stat), whole(pmean), whole(pvar), whole(pcount), whole(sig_h), whole(sig_o),
            part(HOPS), part(G), part(HOPS), part(G), part(G), part(G), wide, wide,
        ],
        out_specs=[
            part(G), part(G), part(HOPS), part(G), part(HOPS), part(G),
            pl.BlockSpec((2, 1, 2 * F, D), lambda h: (0, h, 0, 0)),
        ],
        out_shape=[
            shape(G, bf16), shape(G, bf16), shape(HOPS, bf16), shape(G, f32),
            shape(HOPS, bf16), shape(G, f32),
            jax.ShapeDtypeStruct((2, heads, 2 * F, D), bf16),
        ],
        scratch_shapes=[
            pltpu.VMEM((WIN * T, 2 * F), bf16),
            pltpu.VMEM((2 * F, WIN * T), bf16),
            pltpu.VMEM((G, BAND, T), f32),
            pltpu.VMEM((WIN * T, D), bf16),
            pltpu.VMEM((WIN * T, D), bf16),
            pltpu.VMEM((WIN * T, D), f32),
            pltpu.VMEM((WIN * T, D), f32),
        ],
        compiler_params=pltpu.CompilerParams(
            dimension_semantics=("arbitrary",), vmem_limit_bytes=32 * 1024 * 1024
        ),
        cost_estimate=pl.CostEstimate(
            flops=3_000_000_000, bytes_accessed=12_000_000, transcendentals=1_000_000
        ),
    )(stat, pmean, pvar, pcount, sig_h, sig_o, kh, ko, vh, vo, q, g, wk, wv)


def exchange(value, axes):
    return lax.all_to_all(value, axes, 0, 0)


def copies(value, axes, count):
    return exchange(jnp.broadcast_to(value[None], (count,) + value.shape), axes)


def by_group(rows):
    return jnp.moveaxis(rows.reshape(T, G, -1), 1, 0)


def by_rows(parts):
    return jnp.moveaxis(parts, 0, 1).reshape(1, T, -1)


def on_device(
    queries, key_states, value_states, cotangent, signal, signal_weight,
    embodiment, token_type, earliest, prior_mean, prior_var, prior_count,
):
    XY, ZC, GROUP = ("x", "yh", "yl"), ("z", "c"), ("yl", "c")
    n_x, n_z = lax.axis_size("x"), lax.axis_size("z")
    n_xh = n_x * lax.axis_size("yh")
    n_xy, n_zc = n_xh * lax.axis_size("yl"), n_z * lax.axis_size("c")
    width = queries.shape[2]
    own = lax.axis_index(GROUP)
    up = [(i, i + 1) for i in range(n_z - 1)]
    down = [(i + 1, i) for i in range(n_z - 1)]

    stat = pl.pallas_call(
        stats_kernel, out_shape=jax.ShapeDtypeStruct((n_xy, STAT_ROWS, T), f32)
    )(signal[0], embodiment, token_type)
    stat = pl.pallas_call(
        resum_kernel, out_shape=jax.ShapeDtypeStruct((n_zc, STAT_ROWS, T), f32)
    )(exchange(stat, XY))
    stat = exchange(stat, ZC)

    ko = exchange(by_group(key_states[0]), GROUP)
    vo = exchange(by_group(value_states[0]), GROUP)
    kh = lax.ppermute(ko[1:], "z", up)
    vh = lax.ppermute(vo[1:], "z", up)
    position = lax.axis_index(("z", "yl", "c")) * T + jnp.arange(T, dtype=jnp.int32)
    reach = position[None] - earliest
    info = jnp.concatenate([embodiment, token_type, reach // 16, reach % 16], axis=0)
    packed = jnp.concatenate([signal[0], jnp.pad(info, ((0, 12), (0, 0))).astype(bf16)], axis=0)
    sig_o = copies(packed, GROUP, G)
    sig_h = lax.ppermute(sig_o[1:], "z", up)
    q = exchange(by_group(queries[0]), GROUP)
    g = exchange(by_group(cotangent[0]), GROUP)
    weight = signal_weight.reshape(2 * F, 2 * width)
    share = width // G
    wk = lax.dynamic_slice_in_dim(weight, own * share, share, 1)
    wv = lax.dynamic_slice_in_dim(weight, width + own * share, share, 1)

    att, dq, dkh, dko, dvh, dvo, dw = main_call(
        stat, prior_mean, prior_var, jnp.pad(prior_count, (0, T - E))[None],
        sig_h, sig_o, kh, ko, vh, vo, q, g, wk, wv,
    )

    dw = dw.reshape(n_xh, 2 * F, D)
    dw = jnp.sum(exchange(dw, ("x", "yh")).astype(f32), axis=0)
    dw = exchange(dw.astype(bf16).reshape(n_z, 2 * F // n_z, D), ("z",))
    tokens = T * lax.axis_size(("x", "yh", "z", "yl", "c"))
    dw = (jnp.sum(dw.astype(f32), axis=0) * (1.0 / math.sqrt(tokens))).astype(bf16)
    dw = copies(dw, ("z",), n_z).reshape(2 * F, D)
    dw = copies(dw, XY, n_xy)
    other = lax.ppermute(dw, "c", [(0, 1), (1, 0)])
    first_core = lax.axis_index("c") == 0
    both = jnp.stack([jnp.where(first_core, dw, other), jnp.where(first_core, other, dw)])
    heads = share // D
    both = both.reshape(2, 2, heads, 2, 2 * F, D)
    d_weight = jnp.transpose(both, (4, 1, 3, 0, 2, 5)).reshape(2, F, 2 * width)

    dk_back = lax.ppermute(dkh, "z", down)
    dv_back = lax.ppermute(dvh, "z", down)
    front = ((1, 0), (0, 0), (0, 0))
    dk = (dko + jnp.pad(dk_back, front).astype(f32)).astype(bf16)
    dv = (dvo + jnp.pad(dv_back, front).astype(f32)).astype(bf16)
    return (
        by_rows(exchange(att, GROUP)),
        by_rows(exchange(dq, GROUP)),
        by_rows(exchange(dk, GROUP)),
        by_rows(exchange(dv, GROUP)),
        d_weight,
    )


def solution(mesh):
    split = Mesh(mesh.devices.reshape(4, 2, 8, 2, 2), ("x", "yh", "z", "yl", "c"))
    dp, ctx = ("x", "yh"), ("z", "yl", "c")
    rows = P(dp, ctx, None)
    return jax.shard_map(
        on_device,
        mesh=split,
        in_specs=(rows, rows, rows, rows, rows, P(), P(dp, ctx), P(dp, ctx), P(dp, ctx), P(), P(), P()),
        out_specs=(rows, rows, rows, rows, P()),
        check_vma=False,
    )
```

```python
import math

import jax
import jax.numpy as jnp
from jax import lax
from jax.experimental import pallas as pl
from jax.experimental.pallas import tpu as pltpu
from jax.sharding import Mesh
from jax.sharding import PartitionSpec as P

D = 128
F = 128
E = 16
T = 128
HOPS = 3
HEADS_AT_ONCE = 1
SWAPS = 4
G = 4
BAND = (HOPS + 1) * T
WIN = HOPS + G
STAT_ROWS = 2 * E + 8
SIG_ROWS = T // G
PIECE_ROWS = 2 * T + SIG_ROWS + 16
NORM_EPS = 1e-5
LOG2E = math.log2(math.e)

bf16, f32 = jnp.bfloat16, jnp.float32
NN = (((1,), (0,)), ((), ()))
NT = (((1,), (1,)), ((), ()))
TN = (((0,), (0,)), ((), ()))
SCALAR = pl.BlockSpec(memory_space=pltpu.SMEM)


def dot(a, b, dims=NN):
    return lax.dot_general(a, b, dims, preferred_element_type=f32)


def stats_kernel(sig_ref, emb_ref, typ_ref, *refs):
    out_ref = refs[-1]
    sig = sig_ref[...]
    picked = (lax.broadcasted_iota(jnp.int32, (T, T), 0) == emb_ref[...]) & (typ_ref[...] < 2)
    pick = jnp.where(picked, 1.0, 0.0).astype(bf16)
    square = sig.astype(f32) * sig.astype(f32)
    high = square.astype(bf16)
    low = (square - high.astype(f32)).astype(bf16)
    first = dot(pick[:E], sig)
    second = dot(pick[:E], high) + dot(pick[:E], low)
    counts = dot(jnp.ones((8, T), bf16), pick, NT)
    for copy in range(out_ref.shape[0]):
        out_ref[copy, 0:E] = first
        out_ref[copy, E : 2 * E] = second
        out_ref[copy, 2 * E :] = counts


def resum_kernel(scale, in_ref, *refs):
    out_ref = refs[-1]
    total = in_ref[0].astype(f32)
    for part in range(1, in_ref.shape[0]):
        total = total + in_ref[part].astype(f32)
    total = (total * scale).astype(out_ref.dtype)
    for copy in range(out_ref.shape[0]):
        out_ref[copy] = total


def resum(parts, count, scale=1.0, after=()):
    return pl.pallas_call(
        lambda *refs: resum_kernel(scale, *refs),
        in_specs=[pl.BlockSpec(parts.shape)] + [pl.BlockSpec(memory_space=pl.ANY)] * len(after),
        out_shape=jax.ShapeDtypeStruct((count,) + parts.shape[1:], parts.dtype),
    )(parts, *after)


def columns_of(own_ref, s, width):
    return pl.ds(pl.multiple_of(lax.bitwise_xor(own_ref[0], s) * width, width), width)


def piece_at(refs, s):
    return refs[s] if s < 2 else refs[2].at[s - 2]


def got_at(refs, s):
    return refs[2].at[0] if s == 2 else refs[s]


def pieces_of(shape):
    return 2 * [jax.ShapeDtypeStruct(shape, bf16)] + [jax.ShapeDtypeStruct((2,) + shape, bf16)]


def pack_kernel(own_ref, k_ref, v_ref, q_ref, g_ref, sig_ref, emb_ref, typ_ref, early_ref, *rest):
    kv_refs, qg_refs = rest[:3], rest[3:]
    width = kv_refs[0].shape[1]
    sig = [sig_ref[j * SIG_ROWS : (j + 1) * SIG_ROWS] for j in range(G)]
    reach = own_ref[2] + lax.broadcasted_iota(jnp.int32, (1, T), 1) - early_ref[...]
    lines = (emb_ref[...], typ_ref[...], lax.shift_right_logical(reach, 4), reach & 15)
    info = jnp.concatenate(list(lines) + [jnp.zeros((12, T), jnp.int32)], axis=0)
    info = info.astype(f32).astype(bf16)
    tail = [jnp.concatenate([sig[j], info if j == 0 else jnp.zeros_like(info)], axis=0) for j in range(G)]
    tail = jnp.concatenate(tail, axis=1)
    for s in range(G):
        columns = columns_of(own_ref, s, width)
        kv_ref, qg_ref = piece_at(kv_refs, s), piece_at(qg_refs, s)
        kv_ref[0:T] = k_ref[:, columns]
        kv_ref[T : 2 * T] = v_ref[:, columns]
        kv_ref[2 * T :] = tail
        qg_ref[0:T] = q_ref[:, columns]
        qg_ref[T : 2 * T] = g_ref[:, columns]


def pack(own, *args):
    width = args[0].shape[1] // G
    shapes = pieces_of((PIECE_ROWS, width)) + pieces_of((2 * T, width))
    out = pl.pallas_call(
        pack_kernel,
        in_specs=[SCALAR] + [pl.BlockSpec(a.shape) for a in args],
        out_shape=shapes,
    )(own, *args)
    return out[:3], out[3:]


def line_up_kernel(own_ref, *refs):
    out_ref = refs[-1]
    for s in range(G):
        block = lax.bitwise_xor(own_ref[0], s)

        @pl.when(block > 0)
        def _():
            out_ref[jnp.maximum(block - 1, 0)] = got_at(refs, s)[...]


def line_up(own, pieces, after):
    return pl.pallas_call(
        line_up_kernel,
        in_specs=[SCALAR]
        + [pl.BlockSpec(a.shape) for a in pieces]
        + [pl.BlockSpec(memory_space=pl.ANY)] * len(after),
        out_shape=jax.ShapeDtypeStruct((HOPS,) + pieces[0].shape, bf16),
    )(own, *pieces, *after)


def second_kernel(in_ref, *refs):
    refs[-1][...] = in_ref[1]


def second_of(pair, after):
    return pl.pallas_call(
        second_kernel,
        in_specs=[pl.BlockSpec(pair.shape)] + [pl.BlockSpec(memory_space=pl.ANY)] * len(after),
        out_shape=jax.ShapeDtypeStruct(pair.shape[1:], pair.dtype),
    )(pair, *after)


def unpack_kernel(own_ref, *refs):
    pieces, (a_ref, b_ref) = refs[:G], refs[-2:]
    width = pieces[0].shape[2]
    for s in range(G):
        columns = columns_of(own_ref, s, width)
        piece = got_at(pieces, s)
        a_ref[:, columns] = piece[0]
        b_ref[:, columns] = piece[1]


def unpack(own, pieces, after=()):
    shape = jax.ShapeDtypeStruct((T, pieces[0].shape[2] * G), bf16)
    return pl.pallas_call(
        unpack_kernel,
        in_specs=[SCALAR]
        + [pl.BlockSpec(a.shape) for a in pieces]
        + [pl.BlockSpec(memory_space=pl.ANY)] * len(after),
        out_shape=[shape, shape],
    )(own, *pieces, *after)


def add_kernel(own_ref, mine_ref, back_ref, *out_refs):
    for s in range(G):
        block = lax.bitwise_xor(own_ref[0], s)
        for kv in range(2):

            @pl.when(block == 0)
            def _():
                piece_at(out_refs, s)[kv] = mine_ref[kv, 0].astype(bf16)

            @pl.when(block > 0)
            def _():
                back = back_ref[kv, jnp.maximum(block - 1, 0)].astype(f32)
                piece_at(out_refs, s)[kv] = (mine_ref[kv, block] + back).astype(bf16)


def add_back(own, mine, back):
    return pl.pallas_call(
        add_kernel,
        in_specs=[SCALAR, pl.BlockSpec(mine.shape), pl.BlockSpec(back.shape)],
        out_shape=pieces_of((2, T, mine.shape[3])),
    )(own, mine, back)


def spread_kernel(heads, place_ref, *refs):
    mine_ref, other_refs, out_ref = refs[0], refs[1:-1], refs[-1]
    core, width = place_ref[1], heads * D
    size = other_refs[0].shape[0]
    for half in range(2):
        base = (core if half == 0 else 1 - core) * width
        for j in range(mine_ref.shape[0]):
            kv, h, y_lo = j // (2 * heads), (j // 2) % heads, j % 2
            column = base + ((kv * 2 + y_lo) * 2 * width + h * D)
            part = mine_ref[j] if half == 0 else other_refs[j // size][j % size]
            out_ref[:, pl.ds(pl.multiple_of(column, D), D)] = part


def spread(place, mine, others, heads):
    return pl.pallas_call(
        lambda *refs: spread_kernel(heads, *refs),
        in_specs=[SCALAR] + [pl.BlockSpec(a.shape) for a in (mine, *others)],
        out_shape=jax.ShapeDtypeStruct((2 * F, 2 * mine.shape[0] * D), bf16),
    )(place, mine, *others)


def split3(value):
    high = value.astype(bf16)
    rest = value - high.astype(f32)
    mid = rest.astype(bf16)
    return high, mid, (rest - mid.astype(f32)).astype(bf16)


def prologue(own, stat_ref, pmean_ref, pvar_ref, pcount_ref, sig_refs, stacked_ref, stacked_t_ref, bias_ref):
    stat = stat_ref[0]
    for part in range(1, stat_ref.shape[0]):
        stat = stat + stat_ref[part]
    diag = lax.broadcasted_iota(jnp.int32, (E, T), 0) == lax.broadcasted_iota(jnp.int32, (E, T), 1)
    column = lambda line: jnp.sum(
        jnp.where(diag, jnp.broadcast_to(line, (E, T)), 0.0), axis=1, keepdims=True
    )
    counts, prior, pmean = column(stat[2 * E : 2 * E + 1]), column(pcount_ref[...]), pmean_ref[...]
    total = prior + counts
    mean = (prior * pmean + stat[0:E]) / total
    square = (prior * (pvar_ref[...] + pmean * pmean) + stat[E : 2 * E]) / total
    inv = lax.rsqrt(square - mean * mean + NORM_EPS)
    zero = jnp.zeros_like(inv)
    table = jnp.concatenate(
        [jnp.concatenate([mean, inv, zero], axis=1), jnp.concatenate([mean, zero, inv], axis=1)], axis=0
    )
    pieces = split3(table)
    row = lax.broadcasted_iota(jnp.int32, (2 * E, T), 0)
    key_row = lax.broadcasted_iota(jnp.int32, (BAND, T), 0)
    last = lax.broadcasted_iota(jnp.int32, (BAND, T), 1) + HOPS * T
    for i, ref in enumerate(sig_refs):
        block = i if i < HOPS else HOPS + lax.bitwise_xor(own, i - HOPS)
        tail = ref[0 : SIG_ROWS + 16]
        info = tail[SIG_ROWS:, 0:T].astype(f32)
        sig = jnp.concatenate([tail[0:SIG_ROWS, j * F : (j + 1) * F] for j in range(G)], axis=0)
        code = (info[0:1] + E * info[1:2]).astype(jnp.int32)
        pick = jnp.where(row == code, 1.0, 0.0).astype(bf16)
        per_token = dot(pick, pieces[0], TN) + dot(pick, pieces[1], TN) + dot(pick, pieces[2], TN)
        centred = sig.astype(f32) - per_token[:, 0:F]
        stacked = jnp.concatenate(
            [centred * per_token[:, F : 2 * F], centred * per_token[:, 2 * F :]], axis=1
        )
        stacked_ref[i * T : (i + 1) * T] = stacked.astype(bf16)
        place = pl.ds(i * T if i < HOPS else pl.multiple_of(block * T, T), T)
        stacked_t_ref[:, place] = stacked.T.astype(bf16)
        if i >= HOPS:
            reach = (16.0 * info[2:3] + info[3:4]).astype(jnp.int32)
            visible = (key_row <= last) & (key_row >= last - reach)
            bias_ref[block - HOPS] = jnp.where(visible, 0.0, -1e30)


def main_kernel(own_ref, stat_ref, pmean_ref, pvar_ref, pcount_ref, *refs):
    halo_in, kv_in, refs = refs[0], refs[1 : 1 + G], refs[1 + G :]
    halo_sig, sig_in, refs = refs[0], refs[1 : 1 + G], refs[1 + G :]
    qg_in, w_ref, refs = refs[:G], refs[G], refs[G + 1 :]
    first_out, halo_ref, mine_ref, dw_ref, refs = refs[:3], refs[3], refs[4], refs[5], refs[6:]
    stacked_ref, stacked_t_ref, bias_ref, kv_ref, grad_ref, pair_ref, a_ref, b_ref = refs
    scale = 1.0 / math.sqrt(D)
    own = own_ref[0]

    @pl.when(pl.program_id(0) == 0)
    def _():
        tails = [halo_sig.at[i] for i in range(HOPS)] + [got_at(sig_in, s) for s in range(G)]
        prologue(
            own, stat_ref, pmean_ref, pvar_ref, pcount_ref, tails, stacked_ref, stacked_t_ref, bias_ref
        )

        pair_ref[...] = jnp.zeros_like(pair_ref)

    pieces = [halo_in.at[i] for i in range(HOPS)] + [got_at(kv_in, s) for s in range(G)]
    for head in range(HEADS_AT_ONCE):
        lanes = slice(head * D, (head + 1) * D)
        embed = dot(stacked_ref[...], jnp.concatenate([w_ref[0, :, lanes], w_ref[1, :, lanes]], axis=1))
        for i in range(WIN):
            rows = slice(i * T, (i + 1) * T)
            block = i if i < HOPS else HOPS + lax.bitwise_xor(own, i - HOPS)
            place = pl.ds(i * T if i < HOPS else pl.multiple_of(block * T, T), T)
            raw = jnp.concatenate([pieces[i][0:T, lanes], pieces[i][T : 2 * T, lanes]], axis=1)
            kv_ref[head, place] = (raw.astype(f32) + embed[rows]).astype(bf16)
        for s in range(G):
            block = lax.bitwise_xor(own, s)
            piece = got_at(qg_in, s)
            pair_ref[head, block, 0:T, 0:D] = piece[0:T, lanes]
            pair_ref[head, block, T:, D:] = piece[T : 2 * T, lanes]
        for b in range(G):
            band = slice(b * T, b * T + BAND)
            both = kv_ref[head, band]
            pair = pair_ref[head, b]
            product = dot(both, pair, NT)
            score, dprobs = product[:, :T] * (scale * LOG2E) + bias_ref[b], product[:, T:]
            expo = jnp.exp2(score - jnp.max(score, axis=0, keepdims=True))
            probs = expo * (1.0 / jnp.sum(expo, axis=0, keepdims=True))
            probs_low = probs.astype(bf16)
            inner = jnp.sum(probs * dprobs, axis=0, keepdims=True)
            dscore = (probs * (dprobs - inner)).astype(bf16)
            a_ref[head, b] = dot(probs_low, both[:, D:], TN).astype(bf16)
            b_ref[head, b] = (dot(dscore, both[:, :D], TN) * scale).astype(bf16)
            grad = dot(jnp.concatenate([dscore, probs_low], axis=1), pair)
            old = slice(b * T, b * T + BAND - T)
            new = slice(b * T + BAND - T, b * T + BAND)
            if b == 0:
                grad_ref[head, old] = grad[: BAND - T]
            else:
                grad_ref[head, old] += grad[: BAND - T]
            grad_ref[head, new] = grad[BAND - T :]
        for s in range(G):
            block = lax.bitwise_xor(own, s)
            piece = piece_at(first_out, s)
            piece[0, :, lanes] = a_ref[head, block]
            piece[1, :, lanes] = b_ref[head, block]
        grad = grad_ref[head]
        low = jnp.concatenate([grad[:, :D] * scale, grad[:, D:]], axis=1).astype(bf16)
        for b in range(WIN):
            for kv in range(2):
                part = low[b * T : (b + 1) * T, kv * D : (kv + 1) * D]
                if b < HOPS:
                    halo_ref[kv, b, :, lanes] = part
                else:
                    mine_ref[kv, b - HOPS, :, lanes] = part
        dw = dot(stacked_t_ref[...], low).astype(bf16)
        dw_ref[0, head] = dw[:, :D]
        dw_ref[1, head] = dw[:, D:]


def main_call(own, stat, pmean, pvar, pcount, halo, kv, qg, w):
    width = w.shape[2]
    heads, lanes = width // D, HEADS_AT_ONCE * D
    whole = lambda a: pl.BlockSpec(a.shape, lambda h, own: (0,) * a.ndim)
    rows = pl.BlockSpec((2 * T, lanes), lambda h, own: (0, h))
    third = pl.BlockSpec((1, 2 * T, lanes), lambda h, own: (0, 0, h))
    early = pl.BlockSpec((HOPS, 2 * T, lanes), lambda h, own: (0, 0, h))
    sig = pl.BlockSpec((T, width), lambda h, own: (2, 0))
    third_sig = pl.BlockSpec((1, T, width), lambda h, own: (0, 2, 0))
    early_sig = pl.BlockSpec((HOPS, T, width), lambda h, own: (0, 2, 0))
    got = lambda spec, third: [spec, spec, third, spec]
    grads = lambda n: pl.BlockSpec((2, n, T, lanes), lambda h, own: (0, 0, 0, h))
    per_head = lambda *shape: pltpu.VMEM((HEADS_AT_ONCE,) + shape[:-1], shape[-1])
    out = pl.pallas_call(
        main_kernel,
        grid_spec=pltpu.PrefetchScalarGridSpec(
            num_scalar_prefetch=1,
            grid=(heads // HEADS_AT_ONCE,),
            in_specs=[whole(stat), whole(pmean), whole(pvar), whole(pcount)]
            + [early] + got(rows, third) + [early_sig] + got(sig, third_sig) + got(rows, third)
            + [pl.BlockSpec((2, 2 * F, lanes), lambda h, own: (0, 0, h))],
            out_specs=2 * [pl.BlockSpec((2, T, lanes), lambda h, own: (0, 0, h))]
            + [pl.BlockSpec((2, 2, T, lanes), lambda h, own: (0, 0, 0, h))]
            + [grads(HOPS), grads(G)]
            + [pl.BlockSpec((2, HEADS_AT_ONCE, 2 * F, D), lambda h, own: (0, h, 0, 0))],
            scratch_shapes=[
                pltpu.VMEM((WIN * T, 2 * F), bf16),
                pltpu.VMEM((2 * F, WIN * T), bf16),
                pltpu.VMEM((G, BAND, T), f32),
                per_head(WIN * T, 2 * D, bf16),
                per_head(WIN * T, 2 * D, f32),
                per_head(G, 2 * T, 2 * D, bf16),
                per_head(G, T, D, bf16),
                per_head(G, T, D, bf16),
            ],
        ),
        out_shape=pieces_of((2, T, width))
        + [
            jax.ShapeDtypeStruct((2, HOPS, T, width), bf16),
            jax.ShapeDtypeStruct((2, G, T, width), bf16),
            jax.ShapeDtypeStruct((2, heads, 2 * F, D), bf16),
        ],
        compiler_params=pltpu.CompilerParams(
            dimension_semantics=("arbitrary",), vmem_limit_bytes=56 * 1024 * 1024
        ),
        cost_estimate=pl.CostEstimate(
            flops=3_000_000_000, bytes_accessed=12_000_000, transcendentals=1_000_000
        ),
    )(own, stat, pmean, pvar, pcount, halo, *kv, halo, *kv, *qg, w)
    return out[:3], out[3], out[4], out[5]


def exchange(value, axes):
    return lax.all_to_all(value, axes, 0, 0)


def on_device(
    queries, key_states, value_states, cotangent, signal, signal_weight,
    embodiment, token_type, earliest, prior_mean, prior_var, prior_count,
):
    XY, Z, GROUP, CTX = ("x", "yh", "yl"), ("zh", "zl"), ("yl", "c"), ("zh", "zl", "yl", "c")
    ZC, PARTS, GATHER = Z + ("c",), ("x", "yh", "zl"), ("x", "yh", "yl", "zl")
    n_xy, n_zc, n_z = lax.axis_size(XY), lax.axis_size(ZC), lax.axis_size(Z)
    width = queries.shape[2]
    share = width // G
    place = [lax.axis_index(GROUP), lax.axis_index("c"), lax.axis_index(CTX) * T]
    place = jnp.stack(place).astype(jnp.int32)

    def swap(value):
        return lax.ppermute(value, "c", [(0, 1), (1, 0)])

    def across(pieces):
        return lax.ppermute(pieces[2], "yl", [(0, 1), (1, 0)])

    def regroup(pieces, crossed, after=()):
        second = second_of(crossed, after) if after else crossed[1]
        return [pieces[0], swap(pieces[1]), crossed, swap(second)]

    kv, qg = pack(
        place, key_states[0], value_states[0], queries[0], cotangent[0], signal[0],
        embodiment, token_type, earliest,
    )
    kv, qg = regroup(kv, across(kv)), regroup(qg, across(qg))

    stat = pl.pallas_call(
        stats_kernel,
        in_specs=[pl.BlockSpec((T, F)), pl.BlockSpec((1, T)), pl.BlockSpec((1, T))]
        + [pl.BlockSpec(memory_space=pl.ANY)],
        out_shape=jax.ShapeDtypeStruct((n_zc, STAT_ROWS, T), f32),
    )(signal[0], embodiment, token_type, kv[1])
    stat = exchange(stat, ZC)
    halo = lax.ppermute(line_up(place, kv, [stat]), Z, [(z, z + 1) for z in range(n_z - 1)])
    stat = exchange(resum(stat, n_xy, after=[qg[2]]), XY)

    weight = signal_weight.reshape(2 * F, 2 * width)
    weight = weight.reshape(2 * F, 2, width)
    weight = jnp.moveaxis(lax.dynamic_slice_in_dim(weight, place[0] * share, share, 2), 1, 0)
    first, back, mine, dw = main_call(
        place, stat, prior_mean, prior_var, jnp.pad(prior_count, (0, T - E))[None], halo, kv, qg, weight
    )

    back = lax.ppermute(back, Z, [(z + 1, z) for z in range(n_z - 1)])
    added = add_back(place, mine, back)
    crossed = across(first)

    heads = share // D
    tokens = T * lax.axis_size(("x", "yh") + CTX)
    n_parts = lax.axis_size(PARTS)
    dw = dw.reshape(n_parts, 2 * heads * 2 * F // n_parts, D)
    dw = resum(exchange(dw, PARTS), lax.axis_size("zh"))
    first = regroup(first, crossed, [dw])
    dw = exchange(dw, ("zh",))
    dw = resum(dw, lax.axis_size(GATHER), 1.0 / math.sqrt(tokens), after=[added[0], crossed])
    dw = exchange(dw, GATHER).reshape(n_xy, 2 * F, D)
    d_weight = spread(place, dw, [swap(part) for part in jnp.split(dw, SWAPS)], heads)
    attended, d_queries = unpack(place, first, after=[d_weight])
    d_keys, d_values = unpack(place, regroup(added, across(added), [d_weight]))
    d_weight = d_weight.reshape(2, F, 2 * width)
    return attended[None], d_queries[None], d_keys[None], d_values[None], d_weight


def solution(mesh):
    split = Mesh(mesh.devices.reshape(4, 2, 4, 2, 2, 2), ("x", "yh", "zh", "zl", "yl", "c"))
    dp, ctx = ("x", "yh"), ("zh", "zl", "yl", "c")
    rows = P(dp, ctx, None)
    return jax.shard_map(
        on_device,
        mesh=split,
        in_specs=(rows, rows, rows, rows, rows, P(), P(dp, ctx), P(dp, ctx), P(dp, ctx), P(), P(), P()),
        out_specs=(rows, rows, rows, rows, P()),
        check_vma=False,
    )
```

```python
import math

import jax
import jax.numpy as jnp
from jax import lax
from jax.experimental import pallas as pl
from jax.experimental.pallas import tpu as pltpu
from jax.sharding import Mesh
from jax.sharding import PartitionSpec as P

D = 128
F = 128
E = 16
T = 128
HOPS = 3
HEADS_AT_ONCE = 1
G = 4
BAND = (HOPS + 1) * T
WIN = HOPS + G
STAT_ROWS = 2 * E + 8
SIG_ROWS = T // G
PIECE_ROWS = 2 * T + SIG_ROWS + 16
NORM_EPS = 1e-5
LOG2E = math.log2(math.e)

bf16, f32 = jnp.bfloat16, jnp.float32
NN = (((1,), (0,)), ((), ()))
NT = (((1,), (1,)), ((), ()))
TN = (((0,), (0,)), ((), ()))
SCALAR = pl.BlockSpec(memory_space=pltpu.SMEM)


def takes(microseconds):
    return pl.CostEstimate(flops=0, bytes_accessed=int(microseconds * 3.6e6), transcendentals=0)


def dot(a, b, dims=NN):
    return lax.dot_general(a, b, dims, preferred_element_type=f32)


def stats_kernel(sig_ref, emb_ref, typ_ref, *refs):
    out_ref = refs[-1]
    sig = sig_ref[...]
    picked = (lax.broadcasted_iota(jnp.int32, (T, T), 0) == emb_ref[...]) & (typ_ref[...] < 2)
    pick = jnp.where(picked, 1.0, 0.0).astype(bf16)
    square = sig.astype(f32) * sig.astype(f32)
    high = square.astype(bf16)
    low = (square - high.astype(f32)).astype(bf16)
    first = dot(pick[:E], sig)
    second = dot(pick[:E], high) + dot(pick[:E], low)
    counts = dot(jnp.ones((8, T), bf16), pick, NT)
    for copy in range(out_ref.shape[0]):
        out_ref[copy, 0:E] = first
        out_ref[copy, E : 2 * E] = second
        out_ref[copy, 2 * E :] = counts


def resum_kernel(scale, in_ref, *refs):
    out_ref = refs[-1]
    total = in_ref[0].astype(f32)
    for part in range(1, in_ref.shape[0]):
        total = total + in_ref[part].astype(f32)
    total = (total * scale).astype(out_ref.dtype)
    for copy in range(out_ref.shape[0]):
        out_ref[copy] = total


def resum(parts, count, scale=1.0, after=()):
    return pl.pallas_call(
        lambda *refs: resum_kernel(scale, *refs),
        in_specs=[pl.BlockSpec(parts.shape)] + [pl.BlockSpec(memory_space=pl.ANY)] * len(after),
        cost_estimate=takes(1.9),
        out_shape=jax.ShapeDtypeStruct((count,) + parts.shape[1:], parts.dtype),
    )(parts, *after)


def columns_of(own_ref, s, width):
    return pl.ds(pl.multiple_of(lax.bitwise_xor(own_ref[0], s) * width, width), width)


def piece_at(refs, s):
    return refs[s] if s < 2 else refs[2].at[s - 2]


def got_at(refs, s):
    return refs[2].at[0] if s == 2 else refs[s]


def pieces_of(shape):
    return 2 * [jax.ShapeDtypeStruct(shape, bf16)] + [jax.ShapeDtypeStruct((2,) + shape, bf16)]


def pack_kernel(own_ref, a_ref, b_ref, *refs):
    extra, outs = refs[:-3], refs[-3:]
    width = outs[0].shape[1]
    if extra:
        sig_ref, emb_ref, typ_ref, early_ref = extra
        reach = own_ref[2] + lax.broadcasted_iota(jnp.int32, (1, T), 1) - early_ref[...]
        lines = (emb_ref[...], typ_ref[...], lax.shift_right_logical(reach, 4), reach & 15)
        info = jnp.concatenate(list(lines) + [jnp.zeros((12, T), jnp.int32)], axis=0)
        info = info.astype(f32).astype(bf16)
        tail = []
        for j in range(G):
            sig = sig_ref[j * SIG_ROWS : (j + 1) * SIG_ROWS]
            tail.append(jnp.concatenate([sig, info if j == 0 else jnp.zeros_like(info)], axis=0))
        tail = jnp.concatenate(tail, axis=1)
    for s in range(G):
        columns = columns_of(own_ref, s, width)
        piece = piece_at(outs, s)
        piece[0:T] = a_ref[:, columns]
        piece[T : 2 * T] = b_ref[:, columns]
        if extra:
            piece[2 * T :] = tail


def pack(own, *args):
    rows = PIECE_ROWS if len(args) > 2 else 2 * T
    return pl.pallas_call(
        pack_kernel,
        in_specs=[SCALAR] + [pl.BlockSpec(a.shape) for a in args],
        cost_estimate=takes(2),
        out_shape=pieces_of((rows, args[0].shape[1] // G)),
    )(own, *args)


def line_up_kernel(own_ref, *refs):
    out_ref = refs[-1]
    for s in range(G):
        block = lax.bitwise_xor(own_ref[0], s)

        @pl.when(block > 0)
        def _():
            out_ref[jnp.maximum(block - 1, 0)] = got_at(refs, s)[...]


def line_up(own, pieces, after):
    return pl.pallas_call(
        line_up_kernel,
        in_specs=[SCALAR]
        + [pl.BlockSpec(a.shape) for a in pieces]
        + [pl.BlockSpec(memory_space=pl.ANY)] * len(after),
        cost_estimate=takes(2.4),
        out_shape=jax.ShapeDtypeStruct((HOPS,) + pieces[0].shape, bf16),
    )(own, *pieces, *after)


def second_kernel(in_ref, *refs):
    refs[-1][...] = in_ref[1]


def second_of(pair, after):
    return pl.pallas_call(
        second_kernel,
        in_specs=[pl.BlockSpec(pair.shape)] + [pl.BlockSpec(memory_space=pl.ANY)] * len(after),
        cost_estimate=takes(1.7),
        out_shape=jax.ShapeDtypeStruct(pair.shape[1:], pair.dtype),
    )(pair, *after)


def unpack_kernel(own_ref, *refs):
    pieces, (a_ref, b_ref) = refs[:G], refs[-2:]
    width = pieces[0].shape[2]
    for s in range(G):
        columns = columns_of(own_ref, s, width)
        piece = got_at(pieces, s)
        a_ref[:, columns] = piece[0]
        b_ref[:, columns] = piece[1]


def unpack(own, pieces, after=()):
    shape = jax.ShapeDtypeStruct((T, pieces[0].shape[2] * G), bf16)
    return pl.pallas_call(
        unpack_kernel,
        in_specs=[SCALAR]
        + [pl.BlockSpec(a.shape) for a in pieces]
        + [pl.BlockSpec(memory_space=pl.ANY)] * len(after),
        cost_estimate=takes(2.2),
        out_shape=[shape, shape],
    )(own, *pieces, *after)


def add_kernel(own_ref, mine_ref, back_ref, *out_refs):
    for s in range(G):
        block = lax.bitwise_xor(own_ref[0], s)
        for kv in range(2):

            @pl.when(block == 0)
            def _():
                piece_at(out_refs, s)[kv] = mine_ref[kv, 0].astype(bf16)

            @pl.when(block > 0)
            def _():
                back = back_ref[kv, jnp.maximum(block - 1, 0)].astype(f32)
                piece_at(out_refs, s)[kv] = (mine_ref[kv, block] + back).astype(bf16)


def add_back(own, mine, back):
    return pl.pallas_call(
        add_kernel,
        in_specs=[SCALAR, pl.BlockSpec(mine.shape), pl.BlockSpec(back.shape)],
        cost_estimate=takes(2.7),
        out_shape=pieces_of((2, T, mine.shape[3])),
    )(own, mine, back)


def once(value, after):
    return pl.pallas_call(
        lambda *refs: None,
        in_specs=[pl.BlockSpec(memory_space=pl.ANY)] * (1 + len(after)),
        out_specs=pl.BlockSpec(memory_space=pl.ANY),
        out_shape=jax.ShapeDtypeStruct(value.shape, value.dtype),
        input_output_aliases={0: 0},
    )(value, *after)


def spread_kernel(heads, place_ref, *refs):
    mine_ref, other_refs, out_ref = refs[0], refs[1:-1], refs[-1]
    core, width = place_ref[1], heads * D
    size = other_refs[0].shape[0]
    for half in range(2):
        base = (core if half == 0 else 1 - core) * width
        for j in range(mine_ref.shape[0]):
            kv, h, y_lo = j // (2 * heads), (j // 2) % heads, j % 2
            column = base + ((kv * 2 + y_lo) * 2 * width + h * D)
            part = mine_ref[j] if half == 0 else other_refs[j // size][j % size]
            out_ref[:, pl.ds(pl.multiple_of(column, D), D)] = part


def spread(place, mine, others, heads):
    return pl.pallas_call(
        lambda *refs: spread_kernel(heads, *refs),
        in_specs=[SCALAR]
        + [pl.BlockSpec(a.shape) for a in (mine, *others)],
        cost_estimate=takes(3.4),
        out_shape=jax.ShapeDtypeStruct((2 * F, 2 * mine.shape[0] * D), bf16),
    )(place, mine, *others)


def split3(value):
    high = value.astype(bf16)
    rest = value - high.astype(f32)
    mid = rest.astype(bf16)
    return high, mid, (rest - mid.astype(f32)).astype(bf16)


def prologue(own, stat_ref, pmean_ref, pvar_ref, pcount_ref, sig_refs, stacked_ref, stacked_t_ref, bias_ref):
    stat = stat_ref[0]
    for part in range(1, stat_ref.shape[0]):
        stat = stat + stat_ref[part]
    diag = lax.broadcasted_iota(jnp.int32, (E, T), 0) == lax.broadcasted_iota(jnp.int32, (E, T), 1)
    column = lambda line: jnp.sum(
        jnp.where(diag, jnp.broadcast_to(line, (E, T)), 0.0), axis=1, keepdims=True
    )
    counts, prior, pmean = column(stat[2 * E : 2 * E + 1]), column(pcount_ref[...]), pmean_ref[...]
    total = prior + counts
    mean = (prior * pmean + stat[0:E]) / total
    square = (prior * (pvar_ref[...] + pmean * pmean) + stat[E : 2 * E]) / total
    inv = lax.rsqrt(square - mean * mean + NORM_EPS)
    zero = jnp.zeros_like(inv)
    table = jnp.concatenate(
        [jnp.concatenate([mean, inv, zero], axis=1), jnp.concatenate([mean, zero, inv], axis=1)], axis=0
    )
    pieces = split3(table)
    row = lax.broadcasted_iota(jnp.int32, (2 * E, T), 0)
    key_row = lax.broadcasted_iota(jnp.int32, (BAND, T), 0)
    last = lax.broadcasted_iota(jnp.int32, (BAND, T), 1) + HOPS * T
    for i, ref in enumerate(sig_refs):
        block = i if i < HOPS else HOPS + lax.bitwise_xor(own, i - HOPS)
        tail = ref[0 : SIG_ROWS + 16]
        info = tail[SIG_ROWS:, 0:T].astype(f32)
        sig = jnp.concatenate([tail[0:SIG_ROWS, j * F : (j + 1) * F] for j in range(G)], axis=0)
        code = (info[0:1] + E * info[1:2]).astype(jnp.int32)
        pick = jnp.where(row == code, 1.0, 0.0).astype(bf16)
        per_token = dot(pick, pieces[0], TN) + dot(pick, pieces[1], TN) + dot(pick, pieces[2], TN)
        centred = sig.astype(f32) - per_token[:, 0:F]
        stacked = jnp.concatenate(
            [centred * per_token[:, F : 2 * F], centred * per_token[:, 2 * F :]], axis=1
        )
        stacked_ref[i * T : (i + 1) * T] = stacked.astype(bf16)
        place = pl.ds(i * T if i < HOPS else pl.multiple_of(block * T, T), T)
        stacked_t_ref[:, place] = stacked.T.astype(bf16)
        if i >= HOPS:
            reach = (16.0 * info[2:3] + info[3:4]).astype(jnp.int32)
            visible = (key_row <= last) & (key_row >= last - reach)
            bias_ref[block - HOPS] = jnp.where(visible, 0.0, -1e30)


def main_kernel(own_ref, stat_ref, pmean_ref, pvar_ref, pcount_ref, *refs):
    halo_in, kv_in, refs = refs[0], refs[1 : 1 + G], refs[1 + G :]
    halo_sig, sig_in, refs = refs[0], refs[1 : 1 + G], refs[1 + G :]
    qg_in, w_ref, refs = refs[:G], refs[G], refs[G + 1 :]
    first_out, halo_ref, mine_ref, dw_ref, refs = refs[:3], refs[3], refs[4], refs[5], refs[6:]
    stacked_ref, stacked_t_ref, bias_ref, kv_ref, grad_ref, pair_ref, a_ref, b_ref = refs
    scale = 1.0 / math.sqrt(D)
    own = own_ref[0]

    @pl.when(pl.program_id(0) == 0)
    def _():
        tails = [halo_sig.at[i] for i in range(HOPS)] + [got_at(sig_in, s) for s in range(G)]
        prologue(
            own, stat_ref, pmean_ref, pvar_ref, pcount_ref, tails, stacked_ref, stacked_t_ref, bias_ref
        )

        pair_ref[...] = jnp.zeros_like(pair_ref)

    pieces = [halo_in.at[i] for i in range(HOPS)] + [got_at(kv_in, s) for s in range(G)]
    for head in range(HEADS_AT_ONCE):
        lanes = slice(head * D, (head + 1) * D)
        embed = dot(stacked_ref[...], jnp.concatenate([w_ref[0, :, lanes], w_ref[1, :, lanes]], axis=1))
        for i in range(WIN):
            rows = slice(i * T, (i + 1) * T)
            block = i if i < HOPS else HOPS + lax.bitwise_xor(own, i - HOPS)
            place = pl.ds(i * T if i < HOPS else pl.multiple_of(block * T, T), T)
            raw = jnp.concatenate([pieces[i][0:T, lanes], pieces[i][T : 2 * T, lanes]], axis=1)
            kv_ref[head, place] = (raw.astype(f32) + embed[rows]).astype(bf16)
        for s in range(G):
            block = lax.bitwise_xor(own, s)
            piece = got_at(qg_in, s)
            pair_ref[head, block, 0:T, 0:D] = piece[0:T, lanes]
            pair_ref[head, block, T:, D:] = piece[T : 2 * T, lanes]
        turned = kv_ref[head].T
        for b in range(G):
            band = slice(b * T, b * T + BAND)
            both = kv_ref[head, band]
            pair = pair_ref[head, b]
            halves = [slice(i * BAND // 2, (i + 1) * BAND // 2) for i in range(2)]
            score, dprobs = [], []
            for half in halves:
                product = dot(both[half], pair, NT)
                score.append(product[:, :T] * (scale * LOG2E) + bias_ref[b, half])
                dprobs.append(product[:, T:])
            most = jnp.maximum(*(jnp.max(part, axis=0, keepdims=True) for part in score))
            expo = [jnp.exp2(part - most) for part in score]
            share = 1.0 / sum(jnp.sum(part, axis=0, keepdims=True) for part in expo)
            probs = [part * share for part in expo]
            inner = sum(jnp.sum(p * d, axis=0, keepdims=True) for p, d in zip(probs, dprobs))
            dscore = jnp.concatenate([(p * (d - inner)).astype(bf16) for p, d in zip(probs, dprobs)], axis=0)
            probs_low = jnp.concatenate([p.astype(bf16) for p in probs], axis=0)
            a_ref[head, b] = dot(turned[D:, band], probs_low).astype(bf16).T
            b_ref[head, b] = (dot(turned[:D, band], dscore) * scale).astype(bf16).T
            grad = dot(jnp.concatenate([dscore, probs_low], axis=1), pair)
            old = slice(b * T, b * T + BAND - T)
            new = slice(b * T + BAND - T, b * T + BAND)
            if b == 0:
                grad_ref[head, old] = grad[: BAND - T]
            else:
                grad_ref[head, old] += grad[: BAND - T]
            grad_ref[head, new] = grad[BAND - T :]
        for s in range(G):
            block = lax.bitwise_xor(own, s)
            piece = piece_at(first_out, s)
            piece[0, :, lanes] = a_ref[head, block]
            piece[1, :, lanes] = b_ref[head, block]
        grad = grad_ref[head]
        low = jnp.concatenate([grad[:, :D] * scale, grad[:, D:]], axis=1).astype(bf16)
        for b in range(WIN):
            for kv in range(2):
                part = low[b * T : (b + 1) * T, kv * D : (kv + 1) * D]
                if b < HOPS:
                    halo_ref[kv, b, :, lanes] = part
                else:
                    mine_ref[kv, b - HOPS, :, lanes] = part
        dw = dot(stacked_t_ref[...], low).astype(bf16)
        dw_ref[0, head] = dw[:, :D]
        dw_ref[1, head] = dw[:, D:]


def main_call(own, stat, pmean, pvar, pcount, halo, kv, qg, w):
    width = w.shape[2]
    heads, lanes = width // D, HEADS_AT_ONCE * D
    whole = lambda a: pl.BlockSpec(a.shape, lambda h, own: (0,) * a.ndim)
    rows = pl.BlockSpec((2 * T, lanes), lambda h, own: (0, h))
    third = pl.BlockSpec((1, 2 * T, lanes), lambda h, own: (0, 0, h))
    early = pl.BlockSpec((HOPS, 2 * T, lanes), lambda h, own: (0, 0, h))
    tail = pl.Element(PIECE_ROWS - 2 * T)
    sig = pl.BlockSpec((tail, pl.Element(width)), lambda h, own: (2 * T, 0))
    third_sig = pl.BlockSpec((pl.Element(1), tail, pl.Element(width)), lambda h, own: (0, 2 * T, 0))
    early_sig = pl.BlockSpec((pl.Element(HOPS), tail, pl.Element(width)), lambda h, own: (0, 2 * T, 0))
    got = lambda spec, third: [spec, spec, third, spec]
    grads = lambda n: pl.BlockSpec((2, n, T, lanes), lambda h, own: (0, 0, 0, h))
    per_head = lambda *shape: pltpu.VMEM((HEADS_AT_ONCE,) + shape[:-1], shape[-1])
    out = pl.pallas_call(
        main_kernel,
        grid_spec=pltpu.PrefetchScalarGridSpec(
            num_scalar_prefetch=1,
            grid=(heads // HEADS_AT_ONCE,),
            in_specs=[whole(stat), whole(pmean), whole(pvar), whole(pcount)]
            + [early] + got(rows, third) + [early_sig] + got(sig, third_sig) + got(rows, third)
            + [pl.BlockSpec((2, 2 * F, lanes), lambda h, own: (0, 0, h))],
            out_specs=2 * [pl.BlockSpec((2, T, lanes), lambda h, own: (0, 0, h))]
            + [pl.BlockSpec((2, 2, T, lanes), lambda h, own: (0, 0, 0, h))]
            + [grads(HOPS), grads(G)]
            + [pl.BlockSpec((2, HEADS_AT_ONCE, 2 * F, D), lambda h, own: (0, h, 0, 0))],
            scratch_shapes=[
                pltpu.VMEM((WIN * T, 2 * F), bf16),
                pltpu.VMEM((2 * F, WIN * T), bf16),
                pltpu.VMEM((G, BAND, T), f32),
                per_head(WIN * T, 2 * D, bf16),
                per_head(WIN * T, 2 * D, f32),
                per_head(G, 2 * T, 2 * D, bf16),
                per_head(G, T, D, bf16),
                per_head(G, T, D, bf16),
            ],
        ),
        out_shape=pieces_of((2, T, width))
        + [
            jax.ShapeDtypeStruct((2, HOPS, T, width), bf16),
            jax.ShapeDtypeStruct((2, G, T, width), bf16),
            jax.ShapeDtypeStruct((2, heads, 2 * F, D), bf16),
        ],
        compiler_params=pltpu.CompilerParams(
            dimension_semantics=("arbitrary",), vmem_limit_bytes=56 * 1024 * 1024
        ),
        cost_estimate=takes(15),
    )(own, stat, pmean, pvar, pcount, halo, *kv, halo, *kv, *qg, w)
    return out[:3], out[3], out[4], out[5]


def exchange(value, axes):
    return lax.all_to_all(value, axes, 0, 0)


def on_device(
    queries, key_states, value_states, cotangent, signal, signal_weight,
    embodiment, token_type, earliest, prior_mean, prior_var, prior_count,
):
    XY, Z, GROUP, CTX = ("x", "yh", "yl"), ("zh", "zl"), ("yl", "c"), ("zh", "zl", "yl", "c")
    ZC, PARTS, GATHER = Z + ("c",), ("x", "yh", "zl"), ("x", "yh", "yl", "zl")
    n_xy, n_zc, n_z = lax.axis_size(XY), lax.axis_size(ZC), lax.axis_size(Z)
    width = queries.shape[2]
    share = width // G
    place = [lax.axis_index(GROUP), lax.axis_index("c"), lax.axis_index(CTX) * T]
    place = jnp.stack(place).astype(jnp.int32)

    def swap(value):
        return lax.ppermute(value, "c", [(0, 1), (1, 0)])

    def across(pieces):
        return lax.ppermute(pieces[2], "yl", [(0, 1), (1, 0)])

    def regroup(pieces, crossed, after=()):
        second = second_of(crossed, after) if after else crossed[1]
        return [pieces[0], swap(pieces[1]), crossed, swap(second)]

    kv = pack(place, key_states[0], value_states[0], signal[0], embodiment, token_type, earliest)
    qg = pack(place, queries[0], cotangent[0])
    kv, qg = regroup(kv, across(kv)), regroup(qg, across(qg))

    stat = pl.pallas_call(
        stats_kernel,
        in_specs=[pl.BlockSpec((T, F)), pl.BlockSpec((1, T)), pl.BlockSpec((1, T))]
        + [pl.BlockSpec(memory_space=pl.ANY)],
        cost_estimate=takes(1.6),
        out_shape=jax.ShapeDtypeStruct((n_zc, STAT_ROWS, T), f32),
    )(signal[0], embodiment, token_type, kv[1])
    stat = exchange(stat, ZC)
    halo = lax.ppermute(line_up(place, kv, [stat]), Z, [(z, z + 1) for z in range(n_z - 1)])
    stat = exchange(resum(stat, n_xy, after=[qg[2]]), XY)

    weight = signal_weight.reshape(2 * F, 2 * width)
    weight = weight.reshape(2 * F, 2, width)
    weight = jnp.moveaxis(lax.dynamic_slice_in_dim(weight, place[0] * share, share, 2), 1, 0)
    first, back, mine, dw = main_call(
        place, stat, prior_mean, prior_var, jnp.pad(prior_count, (0, T - E))[None], halo, kv, qg, weight
    )

    back = lax.ppermute(back, Z, [(z + 1, z) for z in range(n_z - 1)])
    added = add_back(place, mine, back)
    crossed, crossed_g = across(first), across(added)

    heads = share // D
    tokens = T * lax.axis_size(("x", "yh") + CTX)
    n_parts = lax.axis_size(PARTS)
    dw = dw.reshape(n_parts, 2 * heads * 2 * F // n_parts, D)
    dw = resum(exchange(dw, PARTS), lax.axis_size("zh"))
    first = regroup(first, crossed, [dw])
    dw = exchange(dw, ("zh",))
    dw = resum(dw, lax.axis_size(GATHER), 1.0 / math.sqrt(tokens), after=[crossed, crossed_g])
    dw = exchange(dw, GATHER).reshape(n_xy, 2 * F, D)
    attended, d_queries = unpack(place, first)
    d_keys, d_values = unpack(place, regroup(added, crossed_g))
    dw = once(dw, [attended, d_keys])
    d_weight = spread(place, dw, [swap(dw)], heads)
    d_weight = d_weight.reshape(2, F, 2 * width)
    return attended[None], d_queries[None], d_keys[None], d_values[None], d_weight


def solution(mesh):
    split = Mesh(mesh.devices.reshape(4, 2, 4, 2, 2, 2), ("x", "yh", "zh", "zl", "yl", "c"))
    dp, ctx = ("x", "yh"), ("zh", "zl", "yl", "c")
    rows = P(dp, ctx, None)
    return jax.shard_map(
        on_device,
        mesh=split,
        in_specs=(rows, rows, rows, rows, rows, P(), P(dp, ctx), P(dp, ctx), P(dp, ctx), P(), P(), P()),
        out_specs=(rows, rows, rows, rows, P()),
        check_vma=False,
    )
```

```python
import math

import jax
import jax.numpy as jnp
from jax import lax
from jax.experimental import pallas as pl
from jax.experimental.pallas import tpu as pltpu
from jax.sharding import Mesh
from jax.sharding import PartitionSpec as P

D = 128
F = 128
E = 16
T = 128
HOPS = 3
HEADS_AT_ONCE = 1
G = 4
BAND = (HOPS + 1) * T
WIN = HOPS + G
STAT_ROWS = 2 * E + 8
SIG_ROWS = T // G
PIECE_ROWS = 2 * T + SIG_ROWS + 16
NORM_EPS = 1e-5
LOG2E = math.log2(math.e)

bf16, f32 = jnp.bfloat16, jnp.float32
NN = (((1,), (0,)), ((), ()))
NT = (((1,), (1,)), ((), ()))
TN = (((0,), (0,)), ((), ()))
SCALAR = pl.BlockSpec(memory_space=pltpu.SMEM)


def takes(microseconds):
    return pl.CostEstimate(flops=0, bytes_accessed=int(microseconds * 3.6e6), transcendentals=0)


def dot(a, b, dims=NN):
    return lax.dot_general(a, b, dims, preferred_element_type=f32)


def stats_kernel(sig_ref, emb_ref, typ_ref, *refs):
    out_ref = refs[-1]
    sig = sig_ref[...]
    picked = (lax.broadcasted_iota(jnp.int32, (T, T), 0) == emb_ref[...]) & (typ_ref[...] < 2)
    pick = jnp.where(picked, 1.0, 0.0).astype(bf16)
    square = sig.astype(f32) * sig.astype(f32)
    high = square.astype(bf16)
    low = (square - high.astype(f32)).astype(bf16)
    first = dot(pick[:E], sig)
    second = dot(pick[:E], high) + dot(pick[:E], low)
    counts = dot(jnp.ones((8, T), bf16), pick, NT)
    for copy in range(out_ref.shape[0]):
        out_ref[copy, 0:E] = first
        out_ref[copy, E : 2 * E] = second
        out_ref[copy, 2 * E :] = counts


def resum_kernel(scale, in_ref, *refs):
    out_ref = refs[-1]
    total = in_ref[0].astype(f32)
    for part in range(1, in_ref.shape[0]):
        total = total + in_ref[part].astype(f32)
    total = (total * scale).astype(out_ref.dtype)
    for copy in range(out_ref.shape[0]):
        out_ref[copy] = total


def resum(parts, count, scale=1.0, after=()):
    return pl.pallas_call(
        lambda *refs: resum_kernel(scale, *refs),
        in_specs=[pl.BlockSpec(parts.shape)] + [pl.BlockSpec(memory_space=pl.ANY)] * len(after),
        cost_estimate=takes(1.9),
        out_shape=jax.ShapeDtypeStruct((count,) + parts.shape[1:], parts.dtype),
    )(parts, *after)


def columns_of(own_ref, s, width):
    return pl.ds(pl.multiple_of(lax.bitwise_xor(own_ref[0], s) * width, width), width)


def piece_at(refs, s):
    return refs[s] if s < 2 else refs[2].at[s - 2]


def got_at(refs, s):
    return refs[2].at[0] if s == 2 else refs[s]


def pieces_of(shape):
    return 2 * [jax.ShapeDtypeStruct(shape, bf16)] + [jax.ShapeDtypeStruct((2,) + shape, bf16)]


def pack_kernel(own_ref, a_ref, b_ref, *refs):
    extra, outs = refs[:-3], refs[-3:]
    width = outs[0].shape[1]
    if extra:
        sig_ref, emb_ref, typ_ref, early_ref = extra
        reach = own_ref[2] + lax.broadcasted_iota(jnp.int32, (1, T), 1) - early_ref[...]
        lines = (emb_ref[...], typ_ref[...], lax.shift_right_logical(reach, 4), reach & 15)
        info = jnp.concatenate(list(lines) + [jnp.zeros((12, T), jnp.int32)], axis=0)
        info = info.astype(f32).astype(bf16)
        tail = []
        for j in range(G):
            sig = sig_ref[j * SIG_ROWS : (j + 1) * SIG_ROWS]
            tail.append(jnp.concatenate([sig, info if j == 0 else jnp.zeros_like(info)], axis=0))
        tail = jnp.concatenate(tail, axis=1)
    for s in range(G):
        columns = columns_of(own_ref, s, width)
        piece = piece_at(outs, s)
        piece[0:T] = a_ref[:, columns]
        piece[T : 2 * T] = b_ref[:, columns]
        if extra:
            piece[2 * T :] = tail


def pack(own, *args):
    rows = PIECE_ROWS if len(args) > 2 else 2 * T
    return pl.pallas_call(
        pack_kernel,
        in_specs=[SCALAR] + [pl.BlockSpec(a.shape) for a in args],
        cost_estimate=takes(2),
        out_shape=pieces_of((rows, args[0].shape[1] // G)),
    )(own, *args)


def line_up_kernel(own_ref, *refs):
    out_ref = refs[-1]
    for s in range(G):
        block = lax.bitwise_xor(own_ref[0], s)

        @pl.when(block > 0)
        def _():
            out_ref[jnp.maximum(block - 1, 0)] = got_at(refs, s)[...]


def line_up(own, pieces, after):
    return pl.pallas_call(
        line_up_kernel,
        in_specs=[SCALAR]
        + [pl.BlockSpec(a.shape) for a in pieces]
        + [pl.BlockSpec(memory_space=pl.ANY)] * len(after),
        cost_estimate=takes(2.4),
        out_shape=jax.ShapeDtypeStruct((HOPS,) + pieces[0].shape, bf16),
    )(own, *pieces, *after)


def second_kernel(in_ref, *refs):
    refs[-1][...] = in_ref[1]


def second_of(pair, after):
    return pl.pallas_call(
        second_kernel,
        in_specs=[pl.BlockSpec(pair.shape)] + [pl.BlockSpec(memory_space=pl.ANY)] * len(after),
        cost_estimate=takes(1.7),
        out_shape=jax.ShapeDtypeStruct(pair.shape[1:], pair.dtype),
    )(pair, *after)


def unpack_kernel(own_ref, *refs):
    width = refs[0].shape[2]
    for pair in range(2):
        pieces, (a_ref, b_ref) = refs[pair * G : (pair + 1) * G], refs[2 * G + 2 * pair :][:2]
        for s in range(G):
            columns = columns_of(own_ref, s, width)
            piece = got_at(pieces, s)
            a_ref[:, columns] = piece[0]
            b_ref[:, columns] = piece[1]


def unpack(own, *pieces):
    shape = jax.ShapeDtypeStruct((T, pieces[0].shape[2] * G), bf16)
    return pl.pallas_call(
        unpack_kernel,
        in_specs=[SCALAR] + [pl.BlockSpec(a.shape) for a in pieces],
        cost_estimate=takes(3.5),
        out_shape=4 * [shape],
    )(own, *pieces)


def add_kernel(own_ref, mine_ref, back_ref, *out_refs):
    for s in range(G):
        block = lax.bitwise_xor(own_ref[0], s)
        for kv in range(2):

            @pl.when(block == 0)
            def _():
                piece_at(out_refs, s)[kv] = mine_ref[kv, 0].astype(bf16)

            @pl.when(block > 0)
            def _():
                back = back_ref[kv, jnp.maximum(block - 1, 0)].astype(f32)
                piece_at(out_refs, s)[kv] = (mine_ref[kv, block] + back).astype(bf16)


def add_back(own, mine, back):
    return pl.pallas_call(
        add_kernel,
        in_specs=[SCALAR, pl.BlockSpec(mine.shape), pl.BlockSpec(back.shape)],
        cost_estimate=takes(2.7),
        out_shape=pieces_of((2, T, mine.shape[3])),
    )(own, mine, back)


def once(value, after):
    return pl.pallas_call(
        lambda *refs: None,
        in_specs=[pl.BlockSpec(memory_space=pl.ANY)] * (1 + len(after)),
        out_specs=pl.BlockSpec(memory_space=pl.ANY),
        out_shape=jax.ShapeDtypeStruct(value.shape, value.dtype),
        input_output_aliases={0: 0},
    )(value, *after)


def spread_kernel(heads, place_ref, *refs):
    mine_ref, other_refs, out_ref = refs[0], refs[1:-1], refs[-1]
    core, width = place_ref[1], heads * D
    size = other_refs[0].shape[0]
    for half in range(2):
        base = (core if half == 0 else 1 - core) * width
        for j in range(mine_ref.shape[0]):
            kv, h, y_lo = j // (2 * heads), (j // 2) % heads, j % 2
            column = base + ((kv * 2 + y_lo) * 2 * width + h * D)
            part = mine_ref[j] if half == 0 else other_refs[j // size][j % size]
            out_ref[:, pl.ds(pl.multiple_of(column, D), D)] = part


def spread(place, mine, others, heads):
    return pl.pallas_call(
        lambda *refs: spread_kernel(heads, *refs),
        in_specs=[SCALAR]
        + [pl.BlockSpec(a.shape) for a in (mine, *others)],
        cost_estimate=takes(3.4),
        out_shape=jax.ShapeDtypeStruct((2 * F, 2 * mine.shape[0] * D), bf16),
    )(place, mine, *others)


def split3(value):
    high = value.astype(bf16)
    rest = value - high.astype(f32)
    mid = rest.astype(bf16)
    return high, mid, (rest - mid.astype(f32)).astype(bf16)


def prologue(own, stat_ref, pmean_ref, pvar_ref, pcount_ref, sig_refs, stacked_ref, stacked_t_ref, bias_ref):
    stat = stat_ref[0]
    for part in range(1, stat_ref.shape[0]):
        stat = stat + stat_ref[part]
    diag = lax.broadcasted_iota(jnp.int32, (E, T), 0) == lax.broadcasted_iota(jnp.int32, (E, T), 1)
    column = lambda line: jnp.sum(
        jnp.where(diag, jnp.broadcast_to(line, (E, T)), 0.0), axis=1, keepdims=True
    )
    counts, prior, pmean = column(stat[2 * E : 2 * E + 1]), column(pcount_ref[...]), pmean_ref[...]
    total = prior + counts
    mean = (prior * pmean + stat[0:E]) / total
    square = (prior * (pvar_ref[...] + pmean * pmean) + stat[E : 2 * E]) / total
    inv = lax.rsqrt(square - mean * mean + NORM_EPS)
    zero = jnp.zeros_like(inv)
    table = jnp.concatenate(
        [jnp.concatenate([mean, inv, zero], axis=1), jnp.concatenate([mean, zero, inv], axis=1)], axis=0
    )
    pieces = split3(table)
    row = lax.broadcasted_iota(jnp.int32, (2 * E, T), 0)
    key_row = lax.broadcasted_iota(jnp.int32, (BAND, T), 0)
    last = lax.broadcasted_iota(jnp.int32, (BAND, T), 1) + HOPS * T
    for i, ref in enumerate(sig_refs):
        block = i if i < HOPS else HOPS + lax.bitwise_xor(own, i - HOPS)
        tail = ref[0 : SIG_ROWS + 16]
        info = tail[SIG_ROWS:, 0:T].astype(f32)
        sig = jnp.concatenate([tail[0:SIG_ROWS, j * F : (j + 1) * F] for j in range(G)], axis=0)
        code = (info[0:1] + E * info[1:2]).astype(jnp.int32)
        pick = jnp.where(row == code, 1.0, 0.0).astype(bf16)
        per_token = dot(pick, pieces[0], TN) + dot(pick, pieces[1], TN) + dot(pick, pieces[2], TN)
        centred = sig.astype(f32) - per_token[:, 0:F]
        stacked = jnp.concatenate(
            [centred * per_token[:, F : 2 * F], centred * per_token[:, 2 * F :]], axis=1
        )
        stacked_ref[i * T : (i + 1) * T] = stacked.astype(bf16)
        place = pl.ds(i * T if i < HOPS else pl.multiple_of(block * T, T), T)
        stacked_t_ref[:, place] = stacked.T.astype(bf16)
        if i >= HOPS:
            reach = (16.0 * info[2:3] + info[3:4]).astype(jnp.int32)
            visible = (key_row <= last) & (key_row >= last - reach)
            bias_ref[block - HOPS] = jnp.where(visible, 0.0, -1e30)


def main_kernel(own_ref, stat_ref, pmean_ref, pvar_ref, pcount_ref, *refs):
    halo_in, kv_in, refs = refs[0], refs[1 : 1 + G], refs[1 + G :]
    halo_sig, sig_in, refs = refs[0], refs[1 : 1 + G], refs[1 + G :]
    qg_in, w_ref, refs = refs[:G], refs[G], refs[G + 1 :]
    first_out, halo_ref, mine_ref, dw_ref, refs = refs[:3], refs[3], refs[4], refs[5], refs[6:]
    stacked_ref, stacked_t_ref, bias_ref, kv_ref, grad_ref, pair_ref, a_ref, b_ref = refs
    scale = 1.0 / math.sqrt(D)
    own = own_ref[0]

    @pl.when(pl.program_id(0) == 0)
    def _():
        tails = [halo_sig.at[i] for i in range(HOPS)] + [got_at(sig_in, s) for s in range(G)]
        prologue(
            own, stat_ref, pmean_ref, pvar_ref, pcount_ref, tails, stacked_ref, stacked_t_ref, bias_ref
        )

        pair_ref[...] = jnp.zeros_like(pair_ref)

    pieces = [halo_in.at[i] for i in range(HOPS)] + [got_at(kv_in, s) for s in range(G)]
    for head in range(HEADS_AT_ONCE):
        lanes = slice(head * D, (head + 1) * D)
        embed = dot(stacked_ref[...], jnp.concatenate([w_ref[0, :, lanes], w_ref[1, :, lanes]], axis=1))
        for i in range(WIN):
            rows = slice(i * T, (i + 1) * T)
            block = i if i < HOPS else HOPS + lax.bitwise_xor(own, i - HOPS)
            place = pl.ds(i * T if i < HOPS else pl.multiple_of(block * T, T), T)
            raw = jnp.concatenate([pieces[i][0:T, lanes], pieces[i][T : 2 * T, lanes]], axis=1)
            kv_ref[head, place] = (raw.astype(f32) + embed[rows]).astype(bf16)
        for s in range(G):
            block = lax.bitwise_xor(own, s)
            piece = got_at(qg_in, s)
            pair_ref[head, block, 0:T, 0:D] = piece[0:T, lanes]
            pair_ref[head, block, T:, D:] = piece[T : 2 * T, lanes]
        turned = kv_ref[head].T
        for b in range(G):
            band = slice(b * T, b * T + BAND)
            both = kv_ref[head, band]
            pair = pair_ref[head, b]
            halves = [slice(i * BAND // 2, (i + 1) * BAND // 2) for i in range(2)]
            score, dprobs = [], []
            for half in halves:
                product = dot(both[half], pair, NT)
                score.append(product[:, :T] * (scale * LOG2E) + bias_ref[b, half])
                dprobs.append(product[:, T:])
            most = jnp.maximum(*(jnp.max(part, axis=0, keepdims=True) for part in score))
            expo = [jnp.exp2(part - most) for part in score]
            share = 1.0 / sum(jnp.sum(part, axis=0, keepdims=True) for part in expo)
            probs = [part * share for part in expo]
            inner = sum(jnp.sum(p * d, axis=0, keepdims=True) for p, d in zip(probs, dprobs))
            dscore = jnp.concatenate([(p * (d - inner)).astype(bf16) for p, d in zip(probs, dprobs)], axis=0)
            probs_low = jnp.concatenate([p.astype(bf16) for p in probs], axis=0)
            a_ref[head, b] = dot(turned[D:, band], probs_low).astype(bf16).T
            b_ref[head, b] = (dot(turned[:D, band], dscore) * scale).astype(bf16).T
            grad = dot(jnp.concatenate([dscore, probs_low], axis=1), pair)
            old = slice(b * T, b * T + BAND - T)
            new = slice(b * T + BAND - T, b * T + BAND)
            if b == 0:
                grad_ref[head, old] = grad[: BAND - T]
            else:
                grad_ref[head, old] += grad[: BAND - T]
            grad_ref[head, new] = grad[BAND - T :]
        for s in range(G):
            block = lax.bitwise_xor(own, s)
            piece = piece_at(first_out, s)
            piece[0, :, lanes] = a_ref[head, block]
            piece[1, :, lanes] = b_ref[head, block]
        grad = grad_ref[head]
        low = jnp.concatenate([grad[:, :D] * scale, grad[:, D:]], axis=1).astype(bf16)
        for b in range(WIN):
            for kv in range(2):
                part = low[b * T : (b + 1) * T, kv * D : (kv + 1) * D]
                if b < HOPS:
                    halo_ref[kv, b, :, lanes] = part
                else:
                    mine_ref[kv, b - HOPS, :, lanes] = part
        dw = dot(stacked_t_ref[...], low).astype(bf16)
        dw_ref[0, head] = dw[:, :D]
        dw_ref[1, head] = dw[:, D:]


def main_call(own, stat, pmean, pvar, pcount, halo, kv, qg, w):
    width = w.shape[2]
    heads, lanes = width // D, HEADS_AT_ONCE * D
    whole = lambda a: pl.BlockSpec(a.shape, lambda h, own: (0,) * a.ndim)
    rows = pl.BlockSpec((2 * T, lanes), lambda h, own: (0, h))
    third = pl.BlockSpec((1, 2 * T, lanes), lambda h, own: (0, 0, h))
    early = pl.BlockSpec((HOPS, 2 * T, lanes), lambda h, own: (0, 0, h))
    tail = pl.Element(PIECE_ROWS - 2 * T)
    sig = pl.BlockSpec((tail, pl.Element(width)), lambda h, own: (2 * T, 0))
    third_sig = pl.BlockSpec((pl.Element(1), tail, pl.Element(width)), lambda h, own: (0, 2 * T, 0))
    early_sig = pl.BlockSpec((pl.Element(HOPS), tail, pl.Element(width)), lambda h, own: (0, 2 * T, 0))
    got = lambda spec, third: [spec, spec, third, spec]
    grads = lambda n: pl.BlockSpec((2, n, T, lanes), lambda h, own: (0, 0, 0, h))
    per_head = lambda *shape: pltpu.VMEM((HEADS_AT_ONCE,) + shape[:-1], shape[-1])
    out = pl.pallas_call(
        main_kernel,
        grid_spec=pltpu.PrefetchScalarGridSpec(
            num_scalar_prefetch=1,
            grid=(heads // HEADS_AT_ONCE,),
            in_specs=[whole(stat), whole(pmean), whole(pvar), whole(pcount)]
            + [early] + got(rows, third) + [early_sig] + got(sig, third_sig) + got(rows, third)
            + [pl.BlockSpec((2, 2 * F, lanes), lambda h, own: (0, 0, h))],
            out_specs=2 * [pl.BlockSpec((2, T, lanes), lambda h, own: (0, 0, h))]
            + [pl.BlockSpec((2, 2, T, lanes), lambda h, own: (0, 0, 0, h))]
            + [grads(HOPS), grads(G)]
            + [pl.BlockSpec((2, HEADS_AT_ONCE, 2 * F, D), lambda h, own: (0, h, 0, 0))],
            scratch_shapes=[
                pltpu.VMEM((WIN * T, 2 * F), bf16),
                pltpu.VMEM((2 * F, WIN * T), bf16),
                pltpu.VMEM((G, BAND, T), f32),
                per_head(WIN * T, 2 * D, bf16),
                per_head(WIN * T, 2 * D, f32),
                per_head(G, 2 * T, 2 * D, bf16),
                per_head(G, T, D, bf16),
                per_head(G, T, D, bf16),
            ],
        ),
        out_shape=pieces_of((2, T, width))
        + [
            jax.ShapeDtypeStruct((2, HOPS, T, width), bf16),
            jax.ShapeDtypeStruct((2, G, T, width), bf16),
            jax.ShapeDtypeStruct((2, heads, 2 * F, D), bf16),
        ],
        compiler_params=pltpu.CompilerParams(
            dimension_semantics=("arbitrary",), vmem_limit_bytes=56 * 1024 * 1024
        ),
        cost_estimate=takes(15),
    )(own, stat, pmean, pvar, pcount, halo, *kv, halo, *kv, *qg, w)
    return out[:3], out[3], out[4], out[5]


def exchange(value, axes):
    return lax.all_to_all(value, axes, 0, 0)


def on_device(
    queries, key_states, value_states, cotangent, signal, signal_weight,
    embodiment, token_type, earliest, prior_mean, prior_var, prior_count,
):
    XY, Z, GROUP, CTX = ("x", "yh", "yl"), ("zh", "zl"), ("yl", "c"), ("zh", "zl", "yl", "c")
    ZC, PARTS, GATHER = Z + ("c",), ("x", "yh", "zl"), ("x", "yh", "yl", "zl")
    n_xy, n_zc, n_z = lax.axis_size(XY), lax.axis_size(ZC), lax.axis_size(Z)
    width = queries.shape[2]
    share = width // G
    place = [lax.axis_index(GROUP), lax.axis_index("c"), lax.axis_index(CTX) * T]
    place = jnp.stack(place).astype(jnp.int32)

    def swap(value):
        return lax.ppermute(value, "c", [(0, 1), (1, 0)])

    def across(pieces):
        return lax.ppermute(pieces[2], "yl", [(0, 1), (1, 0)])

    def regroup(pieces, crossed, after=()):
        second = second_of(crossed, after) if after else crossed[1]
        return [pieces[0], swap(pieces[1]), crossed, swap(second)]

    kv = pack(place, key_states[0], value_states[0], signal[0], embodiment, token_type, earliest)
    qg = pack(place, queries[0], cotangent[0])
    kv, qg = regroup(kv, across(kv)), regroup(qg, across(qg))

    stat = pl.pallas_call(
        stats_kernel,
        in_specs=[pl.BlockSpec((T, F)), pl.BlockSpec((1, T)), pl.BlockSpec((1, T))]
        + [pl.BlockSpec(memory_space=pl.ANY)],
        cost_estimate=takes(1.6),
        out_shape=jax.ShapeDtypeStruct((n_zc, STAT_ROWS, T), f32),
    )(signal[0], embodiment, token_type, kv[1])
    stat = exchange(stat, ZC)
    halo = lax.ppermute(line_up(place, kv, [stat]), Z, [(z, z + 1) for z in range(n_z - 1)])
    stat = exchange(resum(stat, n_xy, after=[qg[2]]), XY)

    weight = signal_weight.reshape(2 * F, 2 * width)
    weight = weight.reshape(2 * F, 2, width)
    weight = jnp.moveaxis(lax.dynamic_slice_in_dim(weight, place[0] * share, share, 2), 1, 0)
    first, back, mine, dw = main_call(
        place, stat, prior_mean, prior_var, jnp.pad(prior_count, (0, T - E))[None], halo, kv, qg, weight
    )

    back = lax.ppermute(back, Z, [(z + 1, z) for z in range(n_z - 1)])
    added = add_back(place, mine, back)
    crossed, crossed_g = across(first), across(added)

    heads = share // D
    tokens = T * lax.axis_size(("x", "yh") + CTX)
    n_parts = lax.axis_size(PARTS)
    dw = dw.reshape(n_parts, 2 * heads * 2 * F // n_parts, D)
    dw = resum(exchange(dw, PARTS), lax.axis_size("zh"))
    first = regroup(first, crossed)
    dw = exchange(dw, ("zh",))
    dw = resum(dw, lax.axis_size(GATHER), 1.0 / math.sqrt(tokens), after=[crossed, crossed_g])
    dw = exchange(dw, GATHER).reshape(n_xy, 2 * F, D)
    attended, d_queries, d_keys, d_values = unpack(place, *first, *regroup(added, crossed_g))
    dw = once(dw, [attended])
    d_weight = spread(place, dw, [swap(dw)], heads)
    d_weight = d_weight.reshape(2, F, 2 * width)
    return attended[None], d_queries[None], d_keys[None], d_values[None], d_weight


def solution(mesh):
    split = Mesh(mesh.devices.reshape(4, 2, 4, 2, 2, 2), ("x", "yh", "zh", "zl", "yl", "c"))
    dp, ctx = ("x", "yh"), ("zh", "zl", "yl", "c")
    rows = P(dp, ctx, None)
    return jax.shard_map(
        on_device,
        mesh=split,
        in_specs=(rows, rows, rows, rows, rows, P(), P(dp, ctx), P(dp, ctx), P(dp, ctx), P(), P(), P()),
        out_specs=(rows, rows, rows, rows, P()),
        check_vma=False,
    )
```
